32 devices in a mesh: grp: 8 (over y, x, core), dp: 4 (over z).
Axes of the slice: x: 2, y: 2, z: 4, core: 2. Of those that a mesh axis runs over, the one named last changes fastest.
Arguments:
- vis_features: bfloat16 [2048, 3200], P(('grp', 'dp')), may hold values from -6 to 6
- vis_gain: float32 [3200], replicated, may hold values from 0.1 to 1.9
- proj_weight: bfloat16 [3200, 8192], P(None, 'dp'), may hold values from -0.109375 to 0.109375
- proj_bias: float32 [8192], P('dp'), may hold values from -3 to 3
- text_embed: bfloat16 [2048, 8192], P('grp', 'dp'), may hold values from -6 to 6
- out_gain: float32 [8192], P('dp'), may hold values from 0.1 to 1.9
- image_counts: int32 [32], P(('grp', 'dp')), may hold values from 1 to 4, as said below
- owner_block: int32 [128], P(('grp', 'dp')), may hold values from 0 to 7, as said below
- offsets: int32 [128], P(('grp', 'dp')), may hold values from 0 to 240, as said below
Outputs:
- hidden: bfloat16 [2048, 8192], P('grp', 'dp')
The draws below stay inside these ranges and needn't reach their ends.
Inputs may be any that keep to these rules, and one draw needn't show every extreme that they name: The live images of a device are its first image_counts slots; some device holds 4 in every draw. `owner_block`: among the image slots of one index of grp (live or not), at most 2 name the same owner, and in every such block some owner is named by exactly 2. `offsets`: the image slots that name one owner (live or not) cover disjoint runs of 16 positions inside its 256 positions.
All inputs are finite; a program needn't handle non-finite values.
Results may differ from the reference program's by a relative error of at most 0.0043.
Values may be sent and summed in bfloat16 or wider, within the bound.
No kernel may reach another device: no remote copies, remote signals or barrier semaphores. Data moves between devices by JAX's collectives and lax.ppermute only.
A program may use at most 64 MiB of HBM per device.

```python
import jax
import jax.numpy as jnp
from jax import lax

V = 3200
D = 8192
PATCH = 16
IMG_CAP = 4
CAP = 2
LEN = 256
IMAGES = 128
TOKENS = 2048


def layout_tables(key):
    blocks = LEN // (CAP * PATCH)
    block_slots = IMAGES // blocks

    def one_block(block_key):
        key_order, key_seats, key_slots = jax.random.split(block_key, 3)
        dest_order = jax.random.permutation(key_order, blocks)
        other_seats = jax.random.permutation(key_seats, (blocks - 1) * CAP)[:block_slots - CAP]
        seat_dest = jnp.concatenate([jnp.full((CAP,), dest_order[0], dtype=jnp.int32), dest_order[1 + other_seats // CAP].astype(jnp.int32)])
        slot_order = jax.random.permutation(key_slots, block_slots)
        return seat_dest[slot_order]
    block_keys = jax.random.split(jax.random.fold_in(key, 7), blocks)
    owners = jax.vmap(one_block)(block_keys).reshape(-1).astype(jnp.int32)
    onehot = (owners[:, None] == jnp.arange(blocks, dtype=jnp.int32)[None, :]).astype(jnp.int32)
    running = jnp.cumsum(onehot, axis=0) - onehot
    rank_in = jnp.sum(running * onehot, axis=1)
    per_owner = jnp.sum(onehot, axis=0)[owners]
    spacing = (LEN - per_owner * PATCH) // (per_owner + 1)
    starts = rank_in * PATCH + (rank_in + 1) * spacing
    return (owners, starts.astype(jnp.int32))


def draw_owner_block(key, part):
    return layout_tables(key)[0]


def draw_offsets(key, part):
    return layout_tables(key)[1]


def draw_image_counts(key, part):
    devices = IMAGES // IMG_CAP
    key_pick, key_chosen = jax.random.split(jax.random.fold_in(key, 11))
    draw_pick = jax.random.randint(key_pick, (devices,), 0, 4)
    counts = jnp.where(draw_pick == 0, IMG_CAP, 1 + draw_pick % max(1, IMG_CAP // 2))
    chosen = jax.random.randint(key_chosen, (), 0, devices)
    counts = jnp.where(jnp.arange(devices) == chosen, IMG_CAP, counts)
    return jnp.clip(counts, 1, IMG_CAP).astype(jnp.int32)


def block_scale(own_key, extent, shards, smallest, high):
    def one(axis_at, shards_of):
        draws = jax.random.uniform(jax.random.fold_in(jax.random.fold_in(own_key, 6), axis_at), (shards_of,), jnp.float32, smallest / len(shards), high / len(shards))
        return jnp.repeat(jnp.exp(draws), extent[axis_at] // shards_of).reshape((-1,) + (1,) * (len(extent) - axis_at - 1))

    factor_of = one(*shards[0])
    for cut in shards[1:]:
        factor_of = factor_of * one(*cut)
    return factor_of


def bell_draw(rng, extent, spread, bound, pieces=(), kind=jnp.bfloat16):
    result = jax.random.normal(rng, extent, jnp.float32) * spread
    if len(pieces) > 0:
        result = block_scale(rng, extent, pieces, -0.22, 0.18) * result
    return jnp.clip(result, min=-bound, max=bound).astype(kind)


def setup_inputs(seed: int = 0) -> dict:
    splits = jax.random.split(jax.random.key(seed), 10)
    vis_features = bell_draw(splits[0], (IMAGES * PATCH, V), 1.0, 6.0, ((0, 32),))
    vis_gain = jnp.clip(1.0 + 0.18 * jax.random.normal(splits[1], (V,), jnp.float32), 0.1, 1.9)
    proj_weight = bell_draw(splits[2], (V, D), V ** -0.5, 0.109375, ((1, 4),))
    proj_bias = bell_draw(splits[3], (D,), 0.5, 3.0, ((0, 4),), jnp.float32)
    text_embed = bell_draw(splits[4], (TOKENS, D), 1.0, 6.0, ((0, 8), (1, 4)))
    out_gain = jnp.clip(1.0 + 0.18 * jax.random.normal(splits[5], (D,), jnp.float32), 0.1, 1.9)
    image_counts = draw_image_counts(jax.random.fold_in(splits[9], 71), 0)
    owner_block = draw_owner_block(jax.random.fold_in(splits[9], 71), 0)
    offsets = draw_offsets(jax.random.fold_in(splits[9], 71), 0)
    return {"vis_features": vis_features, "vis_gain": vis_gain, "proj_weight": proj_weight, "proj_bias": proj_bias, "text_embed": text_embed, "out_gain": out_gain, "image_counts": image_counts, "owner_block": owner_block, "offsets": offsets}


def reference(vis_features, vis_gain, proj_weight, proj_bias, text_embed, out_gain, image_counts, owner_block, offsets):
    vis_rows = vis_features.astype(jnp.float32)
    normed = (vis_rows * lax.rsqrt(lax.optimization_barrier(jnp.mean(vis_rows * vis_rows, axis=-1, keepdims=True)) + 1e-06) * vis_gain).astype(jnp.bfloat16)
    projected = (jnp.dot(normed, proj_weight, preferred_element_type=jnp.float32) + proj_bias).astype(jnp.bfloat16)
    images = owner_block.shape[0]
    slot_index = jnp.arange(images, dtype=jnp.int32) % IMG_CAP
    is_live = slot_index < jnp.repeat(image_counts, IMG_CAP)
    row_start = owner_block * LEN + offsets
    target_rows = row_start[:, None] + jnp.arange(PATCH, dtype=jnp.int32)[None, :]
    target_rows = jnp.where(is_live[:, None], target_rows, TOKENS).reshape(-1).astype(jnp.int32)
    merged = text_embed.at[target_rows].set(projected, mode='drop')
    merged_f = merged.astype(jnp.float32)
    hidden = merged_f * lax.rsqrt(lax.optimization_barrier(jnp.mean(merged_f * merged_f, axis=-1, keepdims=True)) + 1e-05) * out_gain
    return hidden.astype(jnp.bfloat16)
```

```python
import functools

import jax
import jax.numpy as jnp
from jax import lax
from jax.experimental import pallas as pl
from jax.experimental.pallas import tpu as pltpu
from jax.sharding import PartitionSpec as P

EPS_VIS = 1e-06
EPS_OUT = 1e-05
TILE = (8, 128)
F32 = jnp.float32
BF16 = jnp.bfloat16
VMEM = pl.BlockSpec(memory_space=pltpu.VMEM)
SMEM = pl.BlockSpec(memory_space=pltpu.SMEM)
ANY = pl.BlockSpec(memory_space=pl.ANY)


def lanes():
    return lax.broadcasted_iota(jnp.int32, TILE, 1)


def norm_kernel(slots, half, vis, gain, owners, offsets, counts, rows_a, rows_b, info):
    x = vis[...].astype(F32)
    y = x * lax.rsqrt(jnp.mean(x * x, axis=-1, keepdims=True) + EPS_VIS) * gain[...]
    y = y.reshape(slots, 2, half, y.shape[-1])
    rows_a[...] = y[:, 0].reshape(rows_a.shape).astype(BF16)
    rows_b[...] = y[:, 1].reshape(rows_b.shape).astype(BF16)
    lane = lanes()
    tile = jnp.zeros(TILE, jnp.int32)
    for i in range(slots):
        tile = jnp.where(lane == i, owners[i], tile)
        tile = jnp.where(lane == slots + i, jnp.where(i < counts[0], offsets[i], -1), tile)
    for q in range(info.shape[0] // TILE[0]):
        info[q * TILE[0] : (q + 1) * TILE[0], :] = tile


def text_kernel(groups, dp, slots, cap, info, text, squares, seat, start):
    me, row = lax.axis_index("grp"), lax.axis_index("dp")
    lane = lanes()
    tile = jnp.zeros(TILE, F32)
    for c in range(text.shape[0] // 16):
        x = text[c * 16 : (c + 1) * 16, :].astype(F32)
        sums = jnp.sum(x * x, axis=1, keepdims=True)
        tile = jnp.where(lane == 2 * c, sums[:8], tile)
        tile = jnp.where(lane == 2 * c + 1, sums[8:], tile)
    squares[...] = tile
    for o in range(groups):
        start[groups * cap + o] = 0

    def one(image, carry):
        device = image // slots
        owner = info[me * dp + device, image % slots]
        rank = start[groups * cap + owner]
        start[groups * cap + owner] = rank + 1
        seat[(device ^ row) * slots + image % slots] = (owner ^ me) * cap + rank
        return carry

    lax.fori_loop(0, dp * slots, one, 0)

    def other(source, carry):
        def step(image, rank):
            device = source * dp + image // slots
            mine = info[device, image % slots] == me
            place = (source ^ me) * cap + rank

            @pl.when(mine)
            def _():
                start[place] = info[device, slots + image % slots]

            return rank + mine.astype(jnp.int32)

        lax.fori_loop(0, dp * slots, step, jnp.int32(0))
        return carry

    lax.fori_loop(0, groups, other, 0)


def project_kernel(
    groups, cap, half, second, steps, seat, own, a1, b1, a2, b2, a3, weight, bias, *rest
):
    if second:
        before, text_squares, *rest = rest
    outs, (squares, x, placed, partial, sem) = rest[:groups], rest[groups:]
    n = pl.program_id(0)
    row = lax.axis_index("dp")
    rows = own.shape[0]
    images = placed.shape[0] // half

    @pl.when(n == 0)
    def _():
        middle = jnp.logical_or(row == 1, row == 2)
        copies = [pltpu.make_async_copy(own, x.at[0:rows], sem), pltpu.make_async_copy(a1, x.at[rows : 2 * rows], sem)]
        for copy in copies:
            copy.start()

        @pl.when(middle)
        def _():
            pltpu.make_async_copy(b2, x.at[2 * rows : 3 * rows], sem).start()
            pltpu.make_async_copy(b1, x.at[3 * rows : 4 * rows], sem).start()

        @pl.when(jnp.logical_not(middle))
        def _():
            pltpu.make_async_copy(a2, x.at[2 * rows : 3 * rows], sem).start()
            pltpu.make_async_copy(a3, x.at[3 * rows : 4 * rows], sem).start()

        for _ in range(4):
            copies[0].wait()
        partial[...] = jnp.zeros_like(partial)

    y = jnp.dot(x[...], weight[...], preferred_element_type=F32) + bias[...]
    for i in range(images):
        at = pl.multiple_of(seat[i] * half, half)
        placed[pl.ds(at, half), :] = y[i * half : (i + 1) * half, :]
    for k in range(groups):
        part = slice(k * cap * half, (k + 1) * cap * half)
        rounded = placed[part, :].astype(BF16)
        outs[k][...] = rounded
        wide = rounded.astype(F32)
        wide = wide * wide
        total = partial[part, :]
        for c in range(wide.shape[1] // 128):
            total = total + wide[:, c * 128 : (c + 1) * 128]
        partial[part, :] = total

    @pl.when(n == steps - 1)
    def _():
        lane = lanes()
        me = lax.axis_index("grp")
        for k in range(groups):
            owner = me ^ k
            if second:
                tile = before[k * 8 : (k + 1) * 8, :]
            else:
                tile = jnp.zeros(TILE, F32)
            for r in range(cap):
                at = (k * cap + r) * half
                sums = jnp.sum(partial[at : at + half, :], axis=1, keepdims=True)
                tile = jnp.where(lane == (cap if second else 0) + r, sums, tile)
            if not second:
                squares[k * 8 : (k + 1) * 8, :] = tile
            else:
                if k == 0:
                    text = pltpu.roll(text_squares[...], 2 * cap, 1)
                    tile = jnp.where(lane < 2 * cap, tile, text)
                copies = squares.shape[0] // (8 * groups)
                for q in range(copies):
                    at = pl.multiple_of((owner * copies + q) * 8, 8)
                    squares[pl.ds(at, 8), :] = tile


def place_kernel(groups, dp, cap, half, width, start, squares, gain, text, *rest):
    first, second, (out, scale) = rest[:groups], rest[groups : 2 * groups], rest[2 * groups :]

    @pl.when(pl.program_id(0) == 0)
    def _():
        me = lax.axis_index("grp")
        for k in range(groups):
            base = (me ^ k) * (dp * 8)
            total = squares[pl.ds(pl.multiple_of(base, 8), 8), :]
            for d in range(1, dp):
                total = total + squares[pl.ds(pl.multiple_of(base + d * 8, 8), 8), :]
            scale[k * 8 : (k + 1) * 8, :] = lax.rsqrt(total / width + EPS_OUT)

    g = gain[...]
    base = scale[0:8, :]
    for c in range(text.shape[0] // 16):
        at = 2 * cap + 2 * c
        inverse = jnp.concatenate([base[:, at : at + 1], base[:, at + 1 : at + 2]], axis=0)
        x = text[c * 16 : (c + 1) * 16, :].astype(F32)
        out[c * 16 : (c + 1) * 16, :] = (x * inverse * g).astype(BF16)
    for k in range(groups):
        tile = scale[k * 8 : (k + 1) * 8, :]
        for r in range(cap):
            at = start[k * cap + r]

            @pl.when(at >= 0)
            def _():
                part = slice(r * half, (r + 1) * half)
                a = first[k][...].astype(F32)[part] * tile[:, r : r + 1]
                b = second[k][...].astype(F32)[part] * tile[:, cap + r : cap + r + 1]
                rows = (jnp.concatenate([a, b], axis=0) * g).astype(BF16)
                out[pl.ds(pl.multiple_of(at, 2 * half), 2 * half), :] = rows


def project(groups, cap, half, seat, pieces, weight, bias, before=None, text_squares=None, devices=1):
    depth, columns = weight.shape
    block = 256
    steps = columns // block
    second = before is not None
    rows = pieces[0].shape[0]
    whole = lambda a: pl.BlockSpec(a.shape, lambda n: (0,) * a.ndim)
    extra = (before, text_squares) if second else ()
    shape = (devices * 8, 128) if second else (groups * 8, 128)
    return pl.pallas_call(
        functools.partial(project_kernel, groups, cap, half, second, steps),
        grid=(steps,),
        in_specs=[SMEM]
        + [ANY] * len(pieces)
        + [pl.BlockSpec((depth, block), lambda n: (0, n)), pl.BlockSpec((1, block), lambda n: (0, n))]
        + [whole(a) for a in extra],
        out_specs=[pl.BlockSpec((cap * half, block), lambda n: (0, n))] * groups + [pl.BlockSpec(shape, lambda n: (0, 0))],
        out_shape=[jax.ShapeDtypeStruct((cap * half, columns), BF16)] * groups + [jax.ShapeDtypeStruct(shape, F32)],
        scratch_shapes=[
            pltpu.VMEM((4 * rows, depth), BF16),
            pltpu.VMEM((4 * rows, block), F32),
            pltpu.VMEM((4 * rows, 128), F32),
            pltpu.SemaphoreType.DMA,
        ],
        compiler_params=pltpu.CompilerParams(vmem_limit_bytes=32 << 20),
        cost_estimate=pl.CostEstimate(
            flops=8 * rows * depth * columns, bytes_accessed=2 * depth * columns, transcendentals=0
        ),
        name="project",
    )(seat, *pieces, weight, bias, *extra)


def exchange(x):
    pairs = [(0, 1), (1, 0), (2, 3), (3, 2)]
    return lax.ppermute(x, "dp", pairs)


def inner(x):
    return lax.ppermute(x, "dp", [(1, 2), (2, 1), (0, 0), (3, 3)])


def route(groups, parts):
    sent = [
        lax.ppermute(parts[k], "grp", [(i, i ^ k) for i in range(groups)]) for k in range(1, groups)
    ]
    return [parts[0]] + sent


def fast(vis, vis_gain, weight, bias, text, out_gain, counts, owners, offsets):
    groups, dp = lax.axis_size("grp"), lax.axis_size("dp")
    devices = groups * dp
    slots = owners.shape[0]
    per_image = vis.shape[0] // slots
    half = per_image // 2
    seq_len, columns = text.shape
    cap = seq_len // (groups * per_image)
    rows = slots * half
    rows_a, rows_b, info = pl.pallas_call(
        functools.partial(norm_kernel, slots, half),
        in_specs=[VMEM, VMEM, SMEM, SMEM, SMEM],
        out_specs=[VMEM] * 3,
        out_shape=[jax.ShapeDtypeStruct((rows, vis.shape[1]), BF16)] * 2
        + [jax.ShapeDtypeStruct((devices * 8, 128), jnp.int32)],
        name="norm",
    )(vis, vis_gain[None, :], owners, offsets, counts)

    a1, a1_b = exchange(rows_a), exchange(rows_b)
    b1, b1_b = inner(rows_a), inner(rows_b)
    b2, b2_b = inner(a1), inner(a1_b)
    a2, a2_b = exchange(b1), exchange(b1_b)
    a3, a3_b = exchange(b2), exchange(b2_b)
    known = lax.all_to_all(info, ("grp", "dp"), 0, 0, tiled=True)
    known = known.reshape(devices, 8, 128)[:, 0, : 2 * slots]
    text_squares, seat, start = pl.pallas_call(
        functools.partial(text_kernel, groups, dp, slots, cap),
        in_specs=[SMEM, VMEM],
        out_specs=[VMEM, SMEM, SMEM],
        out_shape=[
            jax.ShapeDtypeStruct(TILE, F32),
            jax.ShapeDtypeStruct((dp * slots,), jnp.int32),
            jax.ShapeDtypeStruct((groups * cap + groups,), jnp.int32),
        ],
        name="tables",
    )(known, text)
    bias = bias[None, :]
    *parts_a, squares_a = project(groups, cap, half, seat, (rows_a, a1, b1, a2, b2, a3), weight, bias)
    first = route(groups, parts_a)
    *parts_b, squares = project(
        groups, cap, half, seat, (rows_b, a1_b, b1_b, a2_b, b2_b, a3_b), weight, bias, squares_a, text_squares, devices
    )
    squares = lax.all_to_all(squares, ("grp", "dp"), 0, 0, tiled=True)
    second = route(groups, parts_b)
    block = 1024
    spec = pl.BlockSpec((cap * half, block), lambda n: (0, n))
    return pl.pallas_call(
        functools.partial(place_kernel, groups, dp, cap, half, columns * dp),
        grid=(columns // block,),
        in_specs=[
            SMEM,
            pl.BlockSpec((devices * 8, 128), lambda n: (0, 0)),
            pl.BlockSpec((1, block), lambda n: (0, n)),
            pl.BlockSpec((seq_len, block), lambda n: (0, n)),
        ]
        + [spec] * (2 * groups),
        out_specs=pl.BlockSpec((seq_len, block), lambda n: (0, n)),
        out_shape=jax.ShapeDtypeStruct(text.shape, BF16),
        scratch_shapes=[pltpu.VMEM((groups * 8, 128), F32)],
        compiler_params=pltpu.CompilerParams(vmem_limit_bytes=24 << 20),
        name="place",
    )(start, squares, out_gain[None, :], text, *first, *second)


def general(
    vis_features, vis_gain, proj_weight, proj_bias, text_embed, out_gain, image_counts, owner_block, offsets
):
    groups = lax.axis_size("grp")
    width = proj_weight.shape[1] * lax.axis_size("dp")
    slots_device = owner_block.shape[0]
    per_image = vis_features.shape[0] // slots_device
    columns = proj_weight.shape[1]
    seq_len = text_embed.shape[0]
    capacity = seq_len // (groups * per_image)
    features_f = vis_features.astype(jnp.float32)
    normed = (
        features_f
        * lax.rsqrt(jnp.mean(features_f * features_f, axis=-1, keepdims=True) + EPS_VIS)
        * vis_gain
    ).astype(jnp.bfloat16)
    slot_local = jnp.arange(slots_device, dtype=jnp.int32)
    live_offsets = jnp.where(slot_local < image_counts[0], offsets, -1)
    block_owner, block_offsets = (
        lax.all_gather(owner_block, "dp", axis=0, tiled=True),
        lax.all_gather(live_offsets, "dp", axis=0, tiled=True),
    )
    projected = (
        jnp.dot(
            lax.all_gather(normed, "dp", axis=0, tiled=True),
            proj_weight,
            preferred_element_type=jnp.float32,
        )
        + proj_bias
    ).astype(jnp.bfloat16)
    block_slots = block_owner.shape[0]
    earlier = jnp.arange(block_slots)[:, None] > jnp.arange(block_slots)[None, :]
    same_owner = block_owner[:, None] == block_owner[None, :]
    rank_in = jnp.sum(same_owner & earlier, axis=1)
    bucket = block_owner * capacity + rank_in
    selector = jnp.arange(groups * capacity, dtype=jnp.int32)[:, None] == bucket[None, :]
    flat_rows = projected.reshape(block_slots, per_image * columns)
    bucketed = jnp.dot(
        selector.astype(jnp.bfloat16), flat_rows, preferred_element_type=jnp.float32
    ).astype(jnp.bfloat16)
    bucketed = bucketed.reshape(groups, capacity * per_image * columns)
    bucket_offsets = jnp.max(jnp.where(selector, block_offsets[None, :], -1), axis=1).reshape(
        groups, capacity
    )
    arrived, arrived_offsets = (
        lax.all_to_all(bucketed, "grp", split_axis=0, concat_axis=0, tiled=True),
        lax.all_to_all(bucket_offsets, "grp", split_axis=0, concat_axis=0, tiled=True),
    )
    received = arrived.reshape(groups * capacity * per_image, columns)
    starts = arrived_offsets.reshape(groups * capacity)
    target = jnp.where(
        starts[:, None] >= 0,
        starts[:, None] + jnp.arange(per_image, dtype=jnp.int32)[None, :],
        seq_len,
    )
    target = target.reshape(-1).astype(jnp.int32)
    merged = text_embed.at[target].set(received, mode="drop")
    local_squares = jnp.sum(jnp.square(merged.astype(jnp.float32)), axis=1)
    row_total = lax.psum(local_squares, "dp")
    inverse_rms = lax.rsqrt(row_total / width + EPS_OUT)
    hidden = merged.astype(jnp.float32) * inverse_rms[:, None] * out_gain
    return hidden.astype(jnp.bfloat16)


def on_device(vis, vis_gain, weight, bias, text, out_gain, counts, owners, offsets):
    groups, dp = lax.axis_size("grp"), lax.axis_size("dp")
    per_image = vis.shape[0] // owners.shape[0]
    cap = text.shape[0] // (groups * per_image)
    full = dp * owners.shape[0] == groups * cap and groups * cap * per_image == text.shape[0]
    fits = dp == 4 and groups & (groups - 1) == 0 and per_image == 16 and cap == 2 and text.shape[0] <= 512
    fits = fits and owners.shape[0] % 4 == 0 and weight.shape[1] % 1024 == 0
    form = fast if full and fits else general
    return form(vis, vis_gain, weight, bias, text, out_gain, counts, owners, offsets)


def solution(mesh):
    return jax.shard_map(
        on_device,
        mesh=mesh,
        in_specs=(
            P(("grp", "dp"), None),
            P(),
            P(None, "dp"),
            P("dp"),
            P("grp", "dp"),
            P("dp"),
            P(("grp", "dp")),
            P(("grp", "dp")),
            P(("grp", "dp")),
        ),
        out_specs=P("grp", "dp"),
        check_vma=False,
    )
```

```python
import functools

import jax
import jax.numpy as jnp
from jax import lax
from jax.experimental import pallas as pl
from jax.experimental.pallas import tpu as pltpu
from jax.sharding import PartitionSpec as P

EPS_VIS = 1e-06
EPS_OUT = 1e-05
TILE = (8, 128)
F32 = jnp.float32
BF16 = jnp.bfloat16
VMEM = pl.BlockSpec(memory_space=pltpu.VMEM)
SMEM = pl.BlockSpec(memory_space=pltpu.SMEM)
ANY = pl.BlockSpec(memory_space=pl.ANY)
LIMIT = 16 << 20


def lanes():
    return lax.broadcasted_iota(jnp.int32, TILE, 1)


def tables_kernel(slots, size, text, owners, offsets, counts, squares, info):
    lane = lanes()
    tile = jnp.zeros(TILE, F32)
    for c in range(text.shape[0] // 16):
        x = text[c * 16 : (c + 1) * 16, :].astype(F32)
        sums = jnp.sum(x * x, axis=1, keepdims=True)
        tile = jnp.where(lane == 2 * c, sums[:8], tile)
        tile = jnp.where(lane == 2 * c + 1, sums[8:], tile)
    squares[...] = tile
    row = lax.axis_index("dp")
    lane = lax.broadcasted_iota(jnp.int32, (size, 128), 1)
    for i in range(slots):
        code = jnp.where(i < counts[0], offsets[i] // size + 1, 0)
        known = jnp.where(lane == 0, owners[i], jnp.where(lane == 1, row * slots + i, jnp.where(lane == 2, code, 0)))
        info[i * size : (i + 1) * size, :] = known.astype(F32).astype(BF16)


def hold_kernel(weight, tile, out):
    del weight
    out[...] = tile[...]


def normed(rows, gain):
    x = rows.astype(F32)
    scale = lax.rsqrt(jnp.mean(x * x, axis=-1, keepdims=True) + EPS_VIS)
    return (x * scale * gain).astype(BF16)


def norm_kernel(own, outer, inner, ends, gain, rows):
    row = lax.axis_index("dp")
    middle = jnp.logical_or(row == 1, row == 2)
    g = gain[...].reshape(1, own.shape[1])
    count = own.shape[0]
    rows[0:count] = normed(own[...], g)
    rows[count : 2 * count] = normed(outer[...], g)
    rows[2 * count : 3 * count] = normed(jnp.where(middle, inner[...], ends[...]), g)


def pass_kernel(own, inner, sent):
    row = lax.axis_index("dp")
    sent[...] = jnp.where(jnp.logical_or(row == 1, row == 2), inner[...], own[...])


def project_kernel(groups, cap, size, i0, i1, i2, i3, rows, last, gain, weight, bias, text_squares, *rest):
    *outs, tiles, x = rest
    me = lax.axis_index("grp")
    depth, columns = weight.shape
    known = jnp.concatenate([i0[...], i1[...], i2[...], i3[...]], axis=0)
    total = known.shape[0]
    down = known.astype(F32)
    across = down.T
    owner_down, slot_down = down[:, 0:1], down[:, 1:2]
    owner, slot = across[0:1, :], across[1:2, :]
    earlier = jnp.logical_and(owner_down == owner, slot_down < slot)
    rank = jnp.sum(earlier.astype(F32), axis=0, keepdims=True).astype(jnp.int32) // size
    place = owner.astype(jnp.int32) ^ me
    position = lax.broadcasted_iota(jnp.int32, (1, total), 1) % size
    seat = (place * cap + rank) * size + position
    order = (lax.broadcasted_iota(jnp.int32, (total, total), 0) == seat).astype(BF16)
    codes = jnp.dot(order, known, preferred_element_type=F32)[:, 2:3]
    every = jnp.concatenate([rows[...], normed(last[...], gain[...].reshape(1, depth))], axis=0)
    x[...] = jnp.dot(order, every, preferred_element_type=F32).astype(BF16)
    block = 256
    partial = jnp.zeros((total, 128), F32)
    for n in range(columns // block):
        at = slice(n * block, (n + 1) * block)
        y = jnp.dot(x[...], weight[:, at], preferred_element_type=F32) + bias[:, at]
        y = y.astype(BF16)
        for k in range(groups):
            outs[k][:, at] = y[k * cap * size : (k + 1) * cap * size]
        wide = y.astype(F32)
        wide = wide * wide
        for c in range(block // 128):
            partial = partial + wide[:, c * 128 : (c + 1) * 128]
    lane = lanes()
    sums = jnp.sum(partial, axis=1, keepdims=True)
    copies = tiles.shape[0] // (8 * groups)
    for k in range(groups):
        tile = jnp.zeros(TILE, F32)
        for r in range(cap):
            at = (k * cap + r) * size
            tile = jnp.where(lane == 2 * r, sums[at : at + 8], tile)
            tile = jnp.where(lane == 2 * r + 1, sums[at + 8 : at + 16], tile)
            tile = jnp.where(lane == 2 * cap + r, codes[at : at + 8], tile)
        if k == 0:
            tile = jnp.where(lane < 3 * cap, tile, pltpu.roll(text_squares[...], 3 * cap, 1))
        for q in range(copies):
            tiles[pl.ds(pl.multiple_of(((me ^ k) * copies + q) * 8, 8), 8), :] = tile


def place_kernel(groups, dp, cap, size, width, squares, gain, text, *rest):
    arrived, (out, rows) = rest[:groups], rest[groups:]
    me = lax.axis_index("grp")
    seq_len = text.shape[0]
    total = groups * cap * size
    g = gain[...]
    codes = []
    for k in range(groups):
        base = (me ^ k) * (dp * 8)
        tile = squares[pl.ds(pl.multiple_of(base, 8), 8), :]
        code = tile
        for d in range(1, dp):
            tile = tile + squares[pl.ds(pl.multiple_of(base + d * 8, 8), 8), :]
        scale = lax.rsqrt(tile / width + EPS_OUT)
        if k == 0:
            own = scale
        for r in range(cap):
            inverse = jnp.concatenate([scale[:, 2 * r : 2 * r + 1], scale[:, 2 * r + 1 : 2 * r + 2]], axis=0)
            part = slice(r * size, (r + 1) * size)
            at = (k * cap + r) * size
            rows[at : at + size, :] = (arrived[k][part, :].astype(F32) * inverse * g).astype(BF16)
            codes += [jnp.broadcast_to(code[:, 2 * cap + r : 2 * cap + r + 1], TILE)] * 2
    code = jnp.concatenate(codes, axis=0).T[0:1, :].astype(jnp.int32)
    position = lax.broadcasted_iota(jnp.int32, (1, total), 1) % size
    target = jnp.where(code > 0, (code - 1) * size + position, -1)
    order = (lax.broadcasted_iota(jnp.int32, (seq_len, total), 0) == target).astype(F32)
    covered = jnp.sum(order, axis=1, keepdims=True)
    moved = jnp.dot(order.astype(BF16), rows[...], preferred_element_type=F32)
    for c in range(seq_len // 16):
        at = 3 * cap + 2 * c
        inverse = jnp.concatenate([own[:, at : at + 1], own[:, at + 1 : at + 2]], axis=0)
        part = slice(c * 16, (c + 1) * 16)
        x = text[part, :].astype(F32) * inverse * g
        out[part, :] = jnp.where(covered[part] > 0, moved[part], x).astype(BF16)


def outer(x):
    return lax.ppermute(x, "dp", [(0, 1), (1, 0), (2, 3), (3, 2)])


def inner(x):
    return lax.ppermute(x, "dp", [(1, 2), (2, 1), (0, 0), (3, 3)])


def ends(x):
    return lax.ppermute(x, "dp", [(0, 3), (3, 0), (1, 1), (2, 2)])


def mirror(x):
    return lax.ppermute(x, "dp", [(0, 3), (1, 2), (2, 1), (3, 0)])


def second(x):
    return lax.ppermute(x, "dp", [(0, 2), (1, 3), (2, 0), (3, 1)])


def far(x):
    return lax.ppermute(x, "dp", [(0, 2), (1, 0), (2, 3), (3, 1)])


def route(parts):
    groups = len(parts)
    near = [k for k in range(1, groups) if k & (k - 1) == 0]
    order = near[:0:-1] + [k for k in range(groups - 1, 0, -1) if k not in near] + near[:1]
    arrived = {k: lax.ppermute(parts[k], "grp", [(i, i ^ k) for i in range(groups)]) for k in order}
    return [parts[0]] + [arrived[k] for k in range(1, groups)]


def fast(vis, vis_gain, weight, bias, text, out_gain, counts, owners, offsets):
    groups, dp = lax.axis_size("grp"), lax.axis_size("dp")
    devices = groups * dp
    slots = owners.shape[0]
    size = vis.shape[0] // slots
    seq_len, columns = text.shape
    cap = seq_len // (groups * size)
    depth = vis.shape[1]
    small = pltpu.CompilerParams(vmem_limit_bytes=LIMIT)
    count = slots * size

    x_outer, x_inner = outer(vis), inner(vis)
    text_squares, info = pl.pallas_call(
        functools.partial(tables_kernel, slots, size),
        in_specs=[VMEM, SMEM, SMEM, SMEM],
        out_specs=[VMEM] * 2,
        out_shape=[jax.ShapeDtypeStruct(TILE, F32), jax.ShapeDtypeStruct((count, 128), BF16)],
        compiler_params=small,
        name="tables",
    )(text, owners, offsets, counts)
    late, text_squares = lax.optimization_barrier((vis, text_squares))
    x_ends = ends(late)
    x_inner, x_outer, late = lax.optimization_barrier((x_inner, x_outer, late))
    sent = pl.pallas_call(
        pass_kernel,
        in_specs=[VMEM] * 2,
        out_specs=VMEM,
        out_shape=jax.ShapeDtypeStruct(vis.shape, BF16),
        compiler_params=small,
        name="pass",
    )(late, x_inner)
    x_far = far(sent)
    sent, text_squares = lax.optimization_barrier((sent, text_squares))
    weight = pltpu.with_memory_space_constraint(weight, pltpu.VMEM)
    text_squares = pl.pallas_call(
        hold_kernel,
        in_specs=[ANY, VMEM],
        out_specs=VMEM,
        out_shape=jax.ShapeDtypeStruct(TILE, F32),
        compiler_params=small,
        cost_estimate=pl.CostEstimate(flops=0, bytes_accessed=2 * weight.size, transcendentals=0),
        name="hold",
    )(weight, text_squares)
    x_outer, text_squares = lax.optimization_barrier((x_outer, text_squares))
    known = (info, outer(info), mirror(info), second(info))
    rows = pl.pallas_call(
        norm_kernel,
        in_specs=[VMEM] * 5,
        out_specs=VMEM,
        out_shape=jax.ShapeDtypeStruct((3 * count, depth), BF16),
        compiler_params=small,
        cost_estimate=pl.CostEstimate(flops=0, bytes_accessed=2 * weight.size, transcendentals=0),
        name="norm",
    )(vis, x_outer, x_inner, x_ends, vis_gain)
    *parts, squares = pl.pallas_call(
        functools.partial(project_kernel, groups, cap, size),
        in_specs=[VMEM] * 10,
        out_specs=[VMEM] * (groups + 1),
        out_shape=[jax.ShapeDtypeStruct((cap * size, columns), BF16)] * groups
        + [jax.ShapeDtypeStruct((devices * 8, 128), F32)],
        scratch_shapes=[pltpu.VMEM((dp * slots * size, depth), BF16)],
        compiler_params=small,
        cost_estimate=pl.CostEstimate(
            flops=2 * dp * slots * size * depth * columns, bytes_accessed=2 * depth * columns, transcendentals=0
        ),
        name="project",
    )(*known, rows, x_far, vis_gain, weight, bias[None, :], text_squares)
    squares = lax.all_to_all(squares, ("grp", "dp"), 0, 0, tiled=True)
    arrived = route(parts)
    return pl.pallas_call(
        functools.partial(place_kernel, groups, dp, cap, size, columns * dp),
        in_specs=[VMEM] * (3 + groups),
        out_specs=VMEM,
        out_shape=jax.ShapeDtypeStruct(text.shape, BF16),
        scratch_shapes=[pltpu.VMEM((groups * cap * size, columns), BF16)],
        compiler_params=small,
        name="place",
    )(squares, out_gain[None, :], text, *arrived)


def general(
    vis_features, vis_gain, proj_weight, proj_bias, text_embed, out_gain, image_counts, owner_block, offsets
):
    groups = lax.axis_size("grp")
    width = proj_weight.shape[1] * lax.axis_size("dp")
    slots_device = owner_block.shape[0]
    per_image = vis_features.shape[0] // slots_device
    columns = proj_weight.shape[1]
    seq_len = text_embed.shape[0]
    capacity = seq_len // (groups * per_image)
    features_f = vis_features.astype(jnp.float32)
    normed = (
        features_f
        * lax.rsqrt(jnp.mean(features_f * features_f, axis=-1, keepdims=True) + EPS_VIS)
        * vis_gain
    ).astype(jnp.bfloat16)
    slot_local = jnp.arange(slots_device, dtype=jnp.int32)
    live_offsets = jnp.where(slot_local < image_counts[0], offsets, -1)
    block_owner, block_offsets = (
        lax.all_gather(owner_block, "dp", axis=0, tiled=True),
        lax.all_gather(live_offsets, "dp", axis=0, tiled=True),
    )
    projected = (
        jnp.dot(
            lax.all_gather(normed, "dp", axis=0, tiled=True),
            proj_weight,
            preferred_element_type=jnp.float32,
        )
        + proj_bias
    ).astype(jnp.bfloat16)
    block_slots = block_owner.shape[0]
    earlier = jnp.arange(block_slots)[:, None] > jnp.arange(block_slots)[None, :]
    same_owner = block_owner[:, None] == block_owner[None, :]
    rank_in = jnp.sum(same_owner & earlier, axis=1)
    bucket = block_owner * capacity + rank_in
    selector = jnp.arange(groups * capacity, dtype=jnp.int32)[:, None] == bucket[None, :]
    flat_rows = projected.reshape(block_slots, per_image * columns)
    bucketed = jnp.dot(
        selector.astype(jnp.bfloat16), flat_rows, preferred_element_type=jnp.float32
    ).astype(jnp.bfloat16)
    bucketed = bucketed.reshape(groups, capacity * per_image * columns)
    bucket_offsets = jnp.max(jnp.where(selector, block_offsets[None, :], -1), axis=1).reshape(
        groups, capacity
    )
    arrived, arrived_offsets = (
        lax.all_to_all(bucketed, "grp", split_axis=0, concat_axis=0, tiled=True),
        lax.all_to_all(bucket_offsets, "grp", split_axis=0, concat_axis=0, tiled=True),
    )
    received = arrived.reshape(groups * capacity * per_image, columns)
    starts = arrived_offsets.reshape(groups * capacity)
    target = jnp.where(
        starts[:, None] >= 0,
        starts[:, None] + jnp.arange(per_image, dtype=jnp.int32)[None, :],
        seq_len,
    )
    target = target.reshape(-1).astype(jnp.int32)
    merged = text_embed.at[target].set(received, mode="drop")
    local_squares = jnp.sum(jnp.square(merged.astype(jnp.float32)), axis=1)
    row_total = lax.psum(local_squares, "dp")
    inverse_rms = lax.rsqrt(row_total / width + EPS_OUT)
    hidden = merged.astype(jnp.float32) * inverse_rms[:, None] * out_gain
    return hidden.astype(jnp.bfloat16)


def on_device(vis, vis_gain, weight, bias, text, out_gain, counts, owners, offsets):
    groups, dp = lax.axis_size("grp"), lax.axis_size("dp")
    per_image = vis.shape[0] // owners.shape[0]
    cap = text.shape[0] // (groups * per_image)
    full = dp * owners.shape[0] == groups * cap and groups * cap * per_image == text.shape[0]
    fits = dp == 4 and groups & (groups - 1) == 0 and per_image == 16 and cap == 2 and text.shape[0] <= 512
    fits = fits and owners.shape[0] % 4 == 0 and weight.shape[1] % 1024 == 0
    form = fast if full and fits else general
    return form(vis, vis_gain, weight, bias, text, out_gain, counts, owners, offsets)


def solution(mesh):
    return jax.shard_map(
        on_device,
        mesh=mesh,
        in_specs=(
            P(("grp", "dp"), None),
            P(),
            P(None, "dp"),
            P("dp"),
            P("grp", "dp"),
            P("dp"),
            P(("grp", "dp")),
            P(("grp", "dp")),
            P(("grp", "dp")),
        ),
        out_specs=P("grp", "dp"),
        check_vma=False,
    )
```

```python
import functools

import jax
import jax.numpy as jnp
from jax import lax
from jax.experimental import pallas as pl
from jax.experimental.pallas import tpu as pltpu
from jax.sharding import PartitionSpec as P

EPS_VIS = 1e-06
EPS_OUT = 1e-05
TILE = (8, 128)
F32 = jnp.float32
BF16 = jnp.bfloat16
VMEM = pl.BlockSpec(memory_space=pltpu.VMEM)
SMEM = pl.BlockSpec(memory_space=pltpu.SMEM)
ANY = pl.BlockSpec(memory_space=pl.ANY)
LIMIT = 16 << 20


def lanes():
    return lax.broadcasted_iota(jnp.int32, TILE, 1)


def tables_kernel(slots, size, text, vis, owners, offsets, counts, squares, info, own):
    lane = lanes()
    tile = jnp.zeros(TILE, F32)
    for c in range(text.shape[0] // 16):
        x = text[c * 16 : (c + 1) * 16, :].astype(F32)
        sums = jnp.sum(x * x, axis=1, keepdims=True)
        tile = jnp.where(lane == 2 * c, sums[:8], tile)
        tile = jnp.where(lane == 2 * c + 1, sums[8:], tile)
    squares[...] = tile
    row = lax.axis_index("dp")
    lane = lax.broadcasted_iota(jnp.int32, (size, 128), 1)
    for i in range(slots):
        code = jnp.where(i < counts[0], offsets[i] // size + 1, 0)
        known = jnp.where(lane == 0, owners[i], jnp.where(lane == 1, row * slots + i, jnp.where(lane == 2, code, 0)))
        info[i * size : (i + 1) * size, :] = known.astype(F32).astype(BF16)
    own[...] = vis[...]


def pass_kernel(own, inner, sent):
    row = lax.axis_index("dp")
    sent[...] = jnp.where(jnp.logical_or(row == 1, row == 2), inner[...], own[...])


def hold_kernel(weight, tile, out):
    del weight
    out[...] = tile[...]


def normed(rows, gain):
    x = rows.astype(F32)
    scale = lax.rsqrt(jnp.mean(x * x, axis=-1, keepdims=True) + EPS_VIS)
    return (x * scale * gain).astype(BF16)


def early_kernel(own, outer, inner, ends, gain, weight, bias, y, x):
    row = lax.axis_index("dp")
    middle = jnp.logical_or(row == 1, row == 2)
    depth, columns = weight.shape
    count = own.shape[0]
    g = gain[...].reshape(1, depth)
    x[0:count] = normed(own[...], g)
    x[count : 2 * count] = normed(outer[...], g)
    x[2 * count : 3 * count] = normed(jnp.where(middle, inner[...], ends[...]), g)
    block = 256
    for n in range(columns // block):
        at = slice(n * block, (n + 1) * block)
        y[:, at] = (jnp.dot(x[...], weight[:, at], preferred_element_type=F32) + bias[:, at]).astype(BF16)


def project_kernel(groups, cap, size, i0, i1, i2, i3, last, gain, weight, bias, early, text_squares, *rest):
    *parts, tiles, y, z, codes = rest
    me = lax.axis_index("grp")
    depth, columns = weight.shape
    known = jnp.concatenate([i0[...], i1[...], i2[...], i3[...]], axis=0)
    total = known.shape[0]
    down = known.astype(F32)
    across = down.T
    owner_down, slot_down = down[:, 0:1], down[:, 1:2]
    owner, slot = across[0:1, :], across[1:2, :]
    earlier = jnp.logical_and(owner_down == owner, slot_down < slot)
    rank = jnp.sum(earlier.astype(F32), axis=0, keepdims=True).astype(jnp.int32) // size
    place = owner.astype(jnp.int32) ^ me
    position = lax.broadcasted_iota(jnp.int32, (1, total), 1) % size
    seat = (place * cap + rank) * size + position
    first = position == 0
    image = lax.broadcasted_iota(jnp.int32, (1, total), 1) // size
    seats = [
        pl.multiple_of(jnp.sum(jnp.where(jnp.logical_and(first, image == i), seat, 0)), size)
        for i in range(total // size)
    ]
    x = normed(last[...], gain[...].reshape(1, depth))
    count = last.shape[0]
    for i in range((total - count) // size):
        y[pl.ds(seats[i], size), :] = early[i * size : (i + 1) * size]
    block = 256
    for n in range(columns // block):
        at = slice(n * block, (n + 1) * block)
        z[:, at] = (jnp.dot(x, weight[:, at], preferred_element_type=F32) + bias[:, at]).astype(BF16)
    for i in range(count // size):
        y[pl.ds(seats[(total - count) // size + i], size), :] = z[i * size : (i + 1) * size]
    for i in range(total // size):
        codes[pl.ds(seats[i], size), :] = down[i * size : (i + 1) * size]
    rows = total // len(parts)
    for m, part in enumerate(parts):
        part[...] = y[m * rows : (m + 1) * rows]
    lane = lanes()
    copies = tiles.shape[0] // (8 * groups)
    for k in range(groups):
        tile = jnp.zeros(TILE, F32)
        for r in range(cap):
            at = (k * cap + r) * size
            wide = y[at : at + size, :].astype(F32)
            sums = jnp.sum(wide * wide, axis=1, keepdims=True)
            tile = jnp.where(lane == 2 * r, sums[:8], jnp.where(lane == 2 * r + 1, sums[8:], tile))
            tile = jnp.where(lane == 2 * cap + r, codes[at : at + 8, 2:3], tile)
        if k == 0:
            tile = jnp.where(lane < 3 * cap, tile, pltpu.roll(text_squares[...], 3 * cap, 1))
        for q in range(copies):
            tiles[pl.ds(pl.multiple_of(((me ^ k) * copies + q) * 8, 8), 8), :] = tile


def scale_kernel(groups, dp, cap, width, squares, scales):
    me = lax.axis_index("grp")
    lane = lanes()
    is_code = jnp.logical_and(lane >= 2 * cap, lane < 3 * cap)
    for k in range(groups):
        base = (me ^ k) * (dp * 8)
        tile = squares[pl.ds(pl.multiple_of(base, 8), 8), :]
        code = tile
        for d in range(1, dp):
            tile = tile + squares[pl.ds(pl.multiple_of(base + d * 8, 8), 8), :]
        scales[k * 8 : (k + 1) * 8, :] = jnp.where(is_code, code, lax.rsqrt(tile / width + EPS_OUT))


def pack_kernel(*refs):
    *parts, out = refs
    rows = parts[0].shape[0] // 2
    for n, part in enumerate(parts):
        out[n * rows : (n + 1) * rows, :] = part[rows:, :]


def scaled(cap, size, k, rows, scales, gain):
    scale = scales[k * 8 : (k + 1) * 8, :]
    out = []
    for r in range(cap):
        inverse = jnp.concatenate([scale[:, 2 * r : 2 * r + 1], scale[:, 2 * r + 1 : 2 * r + 2]], axis=0)
        out.append((rows[r * size : (r + 1) * size, :].astype(F32) * inverse * gain).astype(BF16))
    return out


def moves(seq_len, cap, size, senders, scales):
    lane = 2 * cap
    codes = [
        jnp.broadcast_to(scales[k * 8 : (k + 1) * 8, lane + r : lane + r + 1], TILE)
        for k in senders
        for r in range(cap)
        for _ in range(size // 8)
    ]
    code = jnp.concatenate(codes, axis=0).T[0:1, :].astype(jnp.int32)
    position = lax.broadcasted_iota(jnp.int32, code.shape, 1) % size
    target = jnp.where(code > 0, (code - 1) * size + position, -1)
    return (lax.broadcasted_iota(jnp.int32, (seq_len, code.shape[1]), 0) == target).astype(F32)


def base_kernel(groups, cap, size, scales, gain, text, *rest):
    *even, base, order_odd, rows = rest
    seq_len = text.shape[0]
    g = gain[...]
    order = moves(seq_len, cap, size, range(0, groups, 2), scales)
    odd = moves(seq_len, cap, size, range(1, groups, 2), scales)
    order_odd[...] = odd.astype(BF16)
    covered = jnp.sum(order + odd, axis=1, keepdims=True)
    for n, part in enumerate(even):
        for r, x in enumerate(scaled(cap, size, 2 * n, part, scales, g)):
            at = (n * cap + r) * size
            rows[at : at + size, :] = x
    moved = jnp.dot(order.astype(BF16), rows[...], preferred_element_type=F32)
    own = scales[0:8, :]
    for c in range(seq_len // 16):
        at = 3 * cap + 2 * c
        inverse = jnp.concatenate([own[:, at : at + 1], own[:, at + 1 : at + 2]], axis=0)
        part = slice(c * 16, (c + 1) * 16)
        x = text[part, :].astype(F32) * inverse * g
        base[part, :] = jnp.where(covered[part] > 0, moved[part], x).astype(BF16)


def place_kernel(groups, cap, size, scales, gain, odd, base, order, out, rows):
    g = gain[...]
    for n, k in enumerate(range(1, groups, 2)):
        at = n * cap * size
        for r, x in enumerate(scaled(cap, size, k, odd[at : at + cap * size], scales, g)):
            rows[at + r * size : at + (r + 1) * size, :] = x
    moved = jnp.dot(order[...], rows[...], preferred_element_type=F32)
    out[...] = (base[...].astype(F32) + moved).astype(BF16)


def outer(x):
    return lax.ppermute(x, "dp", [(0, 1), (1, 0), (2, 3), (3, 2)])


def inner(x):
    return lax.ppermute(x, "dp", [(1, 2), (2, 1), (0, 0), (3, 3)])


def ends(x):
    return lax.ppermute(x, "dp", [(0, 3), (3, 0), (1, 1), (2, 2)])


def mirror(x):
    return lax.ppermute(x, "dp", [(0, 3), (1, 2), (2, 1), (3, 0)])


def second(x):
    return lax.ppermute(x, "dp", [(0, 2), (1, 3), (2, 0), (3, 1)])


def far(x):
    return lax.ppermute(x, "dp", [(0, 2), (1, 0), (2, 3), (3, 1)])


def across(x, k):
    return lax.ppermute(x, "grp", [(i, i ^ k) for i in range(lax.axis_size("grp"))])


def fast(vis, vis_gain, weight, bias, text, out_gain, counts, owners, offsets):
    groups, dp = lax.axis_size("grp"), lax.axis_size("dp")
    devices = groups * dp
    slots = owners.shape[0]
    size = vis.shape[0] // slots
    seq_len, columns = text.shape
    cap = seq_len // (groups * size)
    depth = vis.shape[1]
    small = pltpu.CompilerParams(vmem_limit_bytes=LIMIT)
    count = slots * size
    tile = jax.ShapeDtypeStruct(TILE, F32)
    bias = bias[None, :]

    x_inner, x_outer = inner(vis), outer(vis)
    text_squares, info, own = pl.pallas_call(
        functools.partial(tables_kernel, slots, size),
        in_specs=[VMEM, VMEM, SMEM, SMEM, SMEM],
        out_specs=[VMEM] * 3,
        out_shape=[tile, jax.ShapeDtypeStruct((count, 128), BF16), jax.ShapeDtypeStruct(vis.shape, BF16)],
        compiler_params=small,
        name="tables",
    )(text, vis, owners, offsets, counts)
    x_ends = ends(own)
    weight = pltpu.with_memory_space_constraint(weight, pltpu.VMEM)
    text_squares = pl.pallas_call(
        hold_kernel,
        in_specs=[ANY, VMEM],
        out_specs=VMEM,
        out_shape=tile,
        compiler_params=small,
        cost_estimate=pl.CostEstimate(flops=0, bytes_accessed=2 * weight.size, transcendentals=0),
        name="hold",
    )(weight, text_squares)
    x_inner, text_squares = lax.optimization_barrier((x_inner, text_squares))
    sent = pl.pallas_call(
        pass_kernel,
        in_specs=[VMEM] * 2,
        out_specs=VMEM,
        out_shape=jax.ShapeDtypeStruct(vis.shape, BF16),
        compiler_params=small,
        name="pass",
    )(own, x_inner)
    sent, x_outer = lax.optimization_barrier((sent, x_outer))
    x_far = far(sent)
    known = (info, outer(info), mirror(info), second(info))
    cost = pl.CostEstimate(
        flops=2 * 3 * count * depth * columns, bytes_accessed=2 * weight.size, transcendentals=0
    )
    early = pl.pallas_call(
        early_kernel,
        in_specs=[VMEM] * 7,
        out_specs=VMEM,
        out_shape=jax.ShapeDtypeStruct((3 * count, columns), BF16),
        scratch_shapes=[pltpu.VMEM((3 * count, depth), BF16)],
        compiler_params=small,
        cost_estimate=cost,
        name="early",
    )(own, x_outer, x_inner, x_ends, vis_gain, weight, bias)
    pairs = groups // 2
    *parts, squares = pl.pallas_call(
        functools.partial(project_kernel, groups, cap, size),
        in_specs=[VMEM] * 10,
        out_specs=[VMEM] * (pairs + 1),
        out_shape=[jax.ShapeDtypeStruct((2 * cap * size, columns), BF16)] * pairs
        + [jax.ShapeDtypeStruct((devices * 8, 128), F32)],
        scratch_shapes=[
            pltpu.VMEM((dp * count, columns), BF16),
            pltpu.VMEM((count, columns), BF16),
            pltpu.VMEM((dp * count, 128), F32),
        ],
        compiler_params=small,
        cost_estimate=cost,
        name="project",
    )(*known, x_far, vis_gain, weight, bias, early, text_squares)
    squares = lax.all_to_all(squares, ("grp", "dp"), 0, 0, tiled=True)
    scales = pl.pallas_call(
        functools.partial(scale_kernel, groups, dp, cap, columns * dp),
        in_specs=[VMEM],
        out_specs=VMEM,
        out_shape=jax.ShapeDtypeStruct((groups * 8, 128), F32),
        compiler_params=small,
        cost_estimate=pl.CostEstimate(flops=0, bytes_accessed=4 * weight.size, transcendentals=0),
        name="scale",
    )(squares)
    even = [parts[0]] + [across(parts[j], 2 * j) for j in range(1, pairs)]
    *even, scales = lax.optimization_barrier((*even, scales))
    arrived = jax.ShapeDtypeStruct((pairs * cap * size, columns), BF16)
    odd = pl.pallas_call(
        pack_kernel, in_specs=[VMEM] * pairs, out_specs=VMEM, out_shape=arrived, compiler_params=small, name="pack"
    )(*even)
    odd = across(odd, 1)
    gain = out_gain[None, :]
    base, order = pl.pallas_call(
        functools.partial(base_kernel, groups, cap, size),
        in_specs=[VMEM] * (3 + pairs),
        out_specs=[VMEM] * 2,
        out_shape=[
            jax.ShapeDtypeStruct(text.shape, BF16),
            jax.ShapeDtypeStruct((seq_len, pairs * cap * size), BF16),
        ],
        scratch_shapes=[pltpu.VMEM(arrived.shape, BF16)],
        compiler_params=small,
        cost_estimate=pl.CostEstimate(flops=0, bytes_accessed=2 * weight.size, transcendentals=0),
        name="base",
    )(scales, gain, text, *even)
    return pl.pallas_call(
        functools.partial(place_kernel, groups, cap, size),
        in_specs=[VMEM] * 5,
        out_specs=VMEM,
        out_shape=jax.ShapeDtypeStruct(text.shape, BF16),
        scratch_shapes=[pltpu.VMEM(arrived.shape, BF16)],
        compiler_params=small,
        name="place",
    )(scales, gain, odd, base, order)


def general(
    vis_features, vis_gain, proj_weight, proj_bias, text_embed, out_gain, image_counts, owner_block, offsets
):
    groups = lax.axis_size("grp")
    width = proj_weight.shape[1] * lax.axis_size("dp")
    slots_device = owner_block.shape[0]
    per_image = vis_features.shape[0] // slots_device
    columns = proj_weight.shape[1]
    seq_len = text_embed.shape[0]
    capacity = seq_len // (groups * per_image)
    features_f = vis_features.astype(jnp.float32)
    normed = (
        features_f
        * lax.rsqrt(jnp.mean(features_f * features_f, axis=-1, keepdims=True) + EPS_VIS)
        * vis_gain
    ).astype(jnp.bfloat16)
    slot_local = jnp.arange(slots_device, dtype=jnp.int32)
    live_offsets = jnp.where(slot_local < image_counts[0], offsets, -1)
    block_owner, block_offsets = (
        lax.all_gather(owner_block, "dp", axis=0, tiled=True),
        lax.all_gather(live_offsets, "dp", axis=0, tiled=True),
    )
    projected = (
        jnp.dot(
            lax.all_gather(normed, "dp", axis=0, tiled=True),
            proj_weight,
            preferred_element_type=jnp.float32,
        )
        + proj_bias
    ).astype(jnp.bfloat16)
    block_slots = block_owner.shape[0]
    earlier = jnp.arange(block_slots)[:, None] > jnp.arange(block_slots)[None, :]
    same_owner = block_owner[:, None] == block_owner[None, :]
    rank_in = jnp.sum(same_owner & earlier, axis=1)
    bucket = block_owner * capacity + rank_in
    selector = jnp.arange(groups * capacity, dtype=jnp.int32)[:, None] == bucket[None, :]
    flat_rows = projected.reshape(block_slots, per_image * columns)
    bucketed = jnp.dot(
        selector.astype(jnp.bfloat16), flat_rows, preferred_element_type=jnp.float32
    ).astype(jnp.bfloat16)
    bucketed = bucketed.reshape(groups, capacity * per_image * columns)
    bucket_offsets = jnp.max(jnp.where(selector, block_offsets[None, :], -1), axis=1).reshape(
        groups, capacity
    )
    arrived, arrived_offsets = (
        lax.all_to_all(bucketed, "grp", split_axis=0, concat_axis=0, tiled=True),
        lax.all_to_all(bucket_offsets, "grp", split_axis=0, concat_axis=0, tiled=True),
    )
    received = arrived.reshape(groups * capacity * per_image, columns)
    starts = arrived_offsets.reshape(groups * capacity)
    target = jnp.where(
        starts[:, None] >= 0,
        starts[:, None] + jnp.arange(per_image, dtype=jnp.int32)[None, :],
        seq_len,
    )
    target = target.reshape(-1).astype(jnp.int32)
    merged = text_embed.at[target].set(received, mode="drop")
    local_squares = jnp.sum(jnp.square(merged.astype(jnp.float32)), axis=1)
    row_total = lax.psum(local_squares, "dp")
    inverse_rms = lax.rsqrt(row_total / width + EPS_OUT)
    hidden = merged.astype(jnp.float32) * inverse_rms[:, None] * out_gain
    return hidden.astype(jnp.bfloat16)


def on_device(vis, vis_gain, weight, bias, text, out_gain, counts, owners, offsets):
    groups, dp = lax.axis_size("grp"), lax.axis_size("dp")
    per_image = vis.shape[0] // owners.shape[0]
    cap = text.shape[0] // (groups * per_image)
    full = dp * owners.shape[0] == groups * cap and groups * cap * per_image == text.shape[0]
    fits = dp == 4 and groups & (groups - 1) == 0 and per_image == 16 and cap == 2 and text.shape[0] <= 512
    fits = fits and owners.shape[0] % 4 == 0 and weight.shape[1] % 1024 == 0
    form = fast if full and fits else general
    return form(vis, vis_gain, weight, bias, text, out_gain, counts, owners, offsets)


def solution(mesh):
    return jax.shard_map(
        on_device,
        mesh=mesh,
        in_specs=(
            P(("grp", "dp"), None),
            P(),
            P(None, "dp"),
            P("dp"),
            P("grp", "dp"),
            P("dp"),
            P(("grp", "dp")),
            P(("grp", "dp")),
            P(("grp", "dp")),
        ),
        out_specs=P("grp", "dp"),
        check_vma=False,
    )
```

```python
import functools

import jax
import jax.numpy as jnp
from jax import lax
from jax.experimental import pallas as pl
from jax.experimental.pallas import tpu as pltpu
from jax.sharding import PartitionSpec as P

EPS_VIS = 1e-06
EPS_OUT = 1e-05
TILE = (8, 128)
F32 = jnp.float32
BF16 = jnp.bfloat16
VMEM = pl.BlockSpec(memory_space=pltpu.VMEM)
SMEM = pl.BlockSpec(memory_space=pltpu.SMEM)
ANY = pl.BlockSpec(memory_space=pl.ANY)
LIMIT = 16 << 20


def lanes():
    return lax.broadcasted_iota(jnp.int32, TILE, 1)


def tables_kernel(slots, size, text, vis, owners, offsets, counts, squares, info, own):
    lane = lanes()
    tile = jnp.zeros(TILE, F32)
    for c in range(text.shape[0] // 16):
        x = text[c * 16 : (c + 1) * 16, :].astype(F32)
        sums = jnp.sum(x * x, axis=1, keepdims=True)
        tile = jnp.where(lane == 2 * c, sums[:8], tile)
        tile = jnp.where(lane == 2 * c + 1, sums[8:], tile)
    squares[...] = tile
    row = lax.axis_index("dp")
    lane = lax.broadcasted_iota(jnp.int32, (size, 128), 1)
    for i in range(slots):
        code = jnp.where(i < counts[0], offsets[i] // size + 1, 0)
        known = jnp.where(lane == 0, owners[i], jnp.where(lane == 1, row * slots + i, jnp.where(lane == 2, code, 0)))
        info[i * size : (i + 1) * size, :] = known.astype(F32).astype(BF16)
    own[...] = vis[...]


def pass_kernel(own, inner, gain, sent, later):
    row = lax.axis_index("dp")
    depth, stretch = inner.shape[1], sent.shape[1]
    rows = jnp.where(jnp.logical_or(row == 1, row == 2), inner[...], own[...])
    rows = normed(rows, gain[...].reshape(1, depth))
    sent[...] = rows[:, :stretch]
    later[...] = rows[:, stretch:]


def hold_kernel(weight, tile, out):
    del weight
    out[...] = tile[...]


def normed(rows, gain):
    x = rows.astype(F32)
    scale = lax.rsqrt(jnp.mean(x * x, axis=-1, keepdims=True) + EPS_VIS)
    return (x * scale * gain).astype(BF16)


def early_kernel(own, outer, inner, ends, gain, weight, bias, y, x):
    row = lax.axis_index("dp")
    middle = jnp.logical_or(row == 1, row == 2)
    depth, columns = weight.shape
    count = own.shape[0]
    g = gain[...].reshape(1, depth)
    x[0:count] = normed(own[...], g)
    x[count : 2 * count] = normed(outer[...], g)
    x[2 * count : 3 * count] = normed(jnp.where(middle, inner[...], ends[...]), g)
    block = 256
    for n in range(columns // block):
        at = slice(n * block, (n + 1) * block)
        y[:, at] = (jnp.dot(x[...], weight[:, at], preferred_element_type=F32) + bias[:, at]).astype(BF16)


def late_kernel(last, weight, bias, total):
    depth = last.shape[1]
    total[...] = jnp.dot(last[...], weight[:depth, :], preferred_element_type=F32) + bias[...]


def project_kernel(groups, cap, size, i0, i1, i2, i3, last, weight, total, early, text_squares, *rest):
    *parts, tiles, y, z, codes = rest
    me = lax.axis_index("grp")
    depth, columns = weight.shape
    stretch = last.shape[1]
    down = jnp.concatenate([i0[...], i1[...], i2[...], i3[...]], axis=0).astype(F32)
    rows = down.shape[0]
    across = down.T
    owner_down, slot_down = down[:, 0:1], down[:, 1:2]
    owner, slot = across[0:1, :], across[1:2, :]
    earlier = jnp.logical_and(owner_down == owner, slot_down < slot)
    rank = jnp.sum(earlier.astype(F32), axis=0, keepdims=True).astype(jnp.int32) // size
    place = owner.astype(jnp.int32) ^ me
    position = lax.broadcasted_iota(jnp.int32, (1, rows), 1) % size
    seat = (place * cap + rank) * size + position
    first = position == 0
    image = lax.broadcasted_iota(jnp.int32, (1, rows), 1) // size
    at = [
        pl.multiple_of(jnp.sum(jnp.where(jnp.logical_and(first, image == i), seat, 0)), size)
        for i in range(rows // size)
    ]
    block = 256
    for n in range(columns // block):
        part = slice(n * block, (n + 1) * block)
        more = jnp.dot(last[...], weight[depth - stretch :, part], preferred_element_type=F32)
        z[:, part] = (total[:, part] + more).astype(BF16)
    count = early.shape[0] // size
    for i in range(rows // size):
        source, n = (early, i) if i < count else (z, i - count)
        y[pl.ds(at[i], size), :] = source[n * size : (n + 1) * size]
        codes[pl.ds(at[i], size), :] = down[i * size : (i + 1) * size]
    chunk = rows // len(parts)
    for m, part in enumerate(parts):
        part[...] = y[m * chunk : (m + 1) * chunk]
    lane = lanes()
    copies = tiles.shape[0] // (8 * groups)
    for k in range(groups):
        tile = jnp.zeros(TILE, F32)
        for r in range(cap):
            start = (k * cap + r) * size
            wide = y[start : start + size, :].astype(F32)
            tile = jnp.where(lane == 2 * cap + r, codes[start : start + 8, 2:3], tile)
            sums = jnp.sum(wide * wide, axis=1, keepdims=True)
            tile = jnp.where(lane == 2 * r, sums[:8], jnp.where(lane == 2 * r + 1, sums[8:], tile))
        if k == 0:
            tile = jnp.where(lane < 3 * cap, tile, pltpu.roll(text_squares[...], 3 * cap, 1))
        for q in range(copies):
            tiles[pl.ds(pl.multiple_of(((me ^ k) * copies + q) * 8, 8), 8), :] = tile


def scale_kernel(groups, dp, cap, width, squares, scales):
    me = lax.axis_index("grp")
    lane = lanes()
    is_code = jnp.logical_and(lane >= 2 * cap, lane < 3 * cap)
    for k in range(groups):
        base = (me ^ k) * (dp * 8)
        tile = squares[pl.ds(pl.multiple_of(base, 8), 8), :]
        code = tile
        for d in range(1, dp):
            tile = tile + squares[pl.ds(pl.multiple_of(base + d * 8, 8), 8), :]
        scales[k * 8 : (k + 1) * 8, :] = jnp.where(is_code, code, lax.rsqrt(tile / width + EPS_OUT))


def pack_kernel(*refs):
    *parts, out = refs
    rows = parts[0].shape[0] // 2
    for n, part in enumerate(parts):
        out[n * rows : (n + 1) * rows, :] = part[rows:, :]


def scaled(cap, size, k, rows, scales, gain):
    scale = scales[k * 8 : (k + 1) * 8, :]
    out = []
    for r in range(cap):
        inverse = jnp.concatenate([scale[:, 2 * r : 2 * r + 1], scale[:, 2 * r + 1 : 2 * r + 2]], axis=0)
        out.append((rows[r * size : (r + 1) * size, :].astype(F32) * inverse * gain).astype(BF16))
    return out


def moves(seq_len, cap, size, senders, scales):
    lane = 2 * cap
    codes = [
        jnp.broadcast_to(scales[k * 8 : (k + 1) * 8, lane + r : lane + r + 1], TILE)
        for k in senders
        for r in range(cap)
        for _ in range(size // 8)
    ]
    code = jnp.concatenate(codes, axis=0).T[0:1, :].astype(jnp.int32)
    position = lax.broadcasted_iota(jnp.int32, code.shape, 1) % size
    target = jnp.where(code > 0, (code - 1) * size + position, -1)
    return (lax.broadcasted_iota(jnp.int32, (seq_len, code.shape[1]), 0) == target).astype(F32)


def base_kernel(groups, cap, size, scales, gain, text, *rest):
    *even, base, order_odd, rows = rest
    seq_len = text.shape[0]
    g = gain[...]
    order = moves(seq_len, cap, size, range(0, groups, 2), scales)
    odd = moves(seq_len, cap, size, range(1, groups, 2), scales)
    order_odd[...] = odd.astype(BF16)
    covered = jnp.sum(order + odd, axis=1, keepdims=True)
    for n, part in enumerate(even):
        for r, x in enumerate(scaled(cap, size, 2 * n, part, scales, g)):
            at = (n * cap + r) * size
            rows[at : at + size, :] = x
    moved = jnp.dot(order.astype(BF16), rows[...], preferred_element_type=F32)
    own = scales[0:8, :]
    for c in range(seq_len // 16):
        at = 3 * cap + 2 * c
        inverse = jnp.concatenate([own[:, at : at + 1], own[:, at + 1 : at + 2]], axis=0)
        part = slice(c * 16, (c + 1) * 16)
        x = text[part, :].astype(F32) * inverse * g
        base[part, :] = jnp.where(covered[part] > 0, moved[part], x).astype(BF16)


def place_kernel(groups, cap, size, scales, gain, odd, base, order, out, rows):
    g = gain[...]
    for n, k in enumerate(range(1, groups, 2)):
        at = n * cap * size
        for r, x in enumerate(scaled(cap, size, k, odd[at : at + cap * size], scales, g)):
            rows[at + r * size : at + (r + 1) * size, :] = x
    moved = jnp.dot(order[...], rows[...], preferred_element_type=F32)
    out[...] = (base[...].astype(F32) + moved).astype(BF16)


def outer(x):
    return lax.ppermute(x, "dp", [(0, 1), (1, 0), (2, 3), (3, 2)])


def inner(x):
    return lax.ppermute(x, "dp", [(1, 2), (2, 1), (0, 0), (3, 3)])


def ends(x):
    return lax.ppermute(x, "dp", [(0, 3), (3, 0), (1, 1), (2, 2)])


def mirror(x):
    return lax.ppermute(x, "dp", [(0, 3), (1, 2), (2, 1), (3, 0)])


def second(x):
    return lax.ppermute(x, "dp", [(0, 2), (1, 3), (2, 0), (3, 1)])


def far(x):
    return lax.ppermute(x, "dp", [(0, 2), (1, 0), (2, 3), (3, 1)])


def across(x, k):
    return lax.ppermute(x, "grp", [(i, i ^ k) for i in range(lax.axis_size("grp"))])


def fast(vis, vis_gain, weight, bias, text, out_gain, counts, owners, offsets):
    groups, dp = lax.axis_size("grp"), lax.axis_size("dp")
    devices = groups * dp
    slots = owners.shape[0]
    size = vis.shape[0] // slots
    seq_len, columns = text.shape
    cap = seq_len // (groups * size)
    depth = vis.shape[1]
    small = pltpu.CompilerParams(vmem_limit_bytes=LIMIT)
    count = slots * size
    tile = jax.ShapeDtypeStruct(TILE, F32)
    bias = bias[None, :]

    x_inner, x_outer = inner(vis), outer(vis)
    text_squares, info, own = pl.pallas_call(
        functools.partial(tables_kernel, slots, size),
        in_specs=[VMEM, VMEM, SMEM, SMEM, SMEM],
        out_specs=[VMEM] * 3,
        out_shape=[tile, jax.ShapeDtypeStruct((count, 128), BF16), jax.ShapeDtypeStruct(vis.shape, BF16)],
        compiler_params=small,
        name="tables",
    )(text, vis, owners, offsets, counts)
    x_ends = ends(vis)
    weight = pltpu.with_memory_space_constraint(weight, pltpu.VMEM)
    text_squares = pl.pallas_call(
        hold_kernel,
        in_specs=[ANY, VMEM],
        out_specs=VMEM,
        out_shape=tile,
        compiler_params=small,
        cost_estimate=pl.CostEstimate(flops=0, bytes_accessed=2 * weight.size, transcendentals=0),
        name="hold",
    )(weight, text_squares)
    x_inner, text_squares = lax.optimization_barrier((x_inner, text_squares))
    stretches = depth // 3 // 128 * 128
    stretches = (depth - stretches, stretches)
    stretch = depth // 3 // 128 * 128
    sent, later = pl.pallas_call(
        pass_kernel,
        in_specs=[VMEM] * 3,
        out_specs=[VMEM] * 2,
        out_shape=[jax.ShapeDtypeStruct((count, n), BF16) for n in (depth - stretch, stretch)],
        compiler_params=small,
        name="pass",
    )(own, x_inner, vis_gain)
    sent, later, x_outer = lax.optimization_barrier((sent, later, x_outer))
    last_a = far(sent)
    known = (info, outer(info), mirror(info), second(info))
    last_b = far(later)
    cost = pl.CostEstimate(
        flops=2 * 3 * count * depth * columns, bytes_accessed=2 * weight.size, transcendentals=0
    )
    early = pl.pallas_call(
        early_kernel,
        in_specs=[VMEM] * 7,
        out_specs=VMEM,
        out_shape=jax.ShapeDtypeStruct((3 * count, columns), BF16),
        scratch_shapes=[pltpu.VMEM((3 * count, depth), BF16)],
        compiler_params=small,
        cost_estimate=cost,
        name="early",
    )(own, x_outer, x_inner, x_ends, vis_gain, weight, bias)
    pairs = groups // 2
    total = pl.pallas_call(
        late_kernel,
        in_specs=[VMEM] * 3,
        out_specs=VMEM,
        out_shape=jax.ShapeDtypeStruct((count, columns), F32),
        compiler_params=small,
        cost_estimate=cost,
        name="late",
    )(last_a, weight, bias)
    *parts, squares = pl.pallas_call(
        functools.partial(project_kernel, groups, cap, size),
        in_specs=[VMEM] * 9,
        out_specs=[VMEM] * (pairs + 1),
        out_shape=[jax.ShapeDtypeStruct((2 * cap * size, columns), BF16)] * pairs
        + [jax.ShapeDtypeStruct((devices * 8, 128), F32)],
        scratch_shapes=[
            pltpu.VMEM((dp * count, columns), BF16),
            pltpu.VMEM((count, columns), BF16),
            pltpu.VMEM((dp * count, 128), F32),
        ],
        compiler_params=small,
        cost_estimate=cost,
        name="project",
    )(*known, last_b, weight, total, early, text_squares)
    squares = lax.all_to_all(squares, ("grp", "dp"), 0, 0, tiled=True)
    scales = pl.pallas_call(
        functools.partial(scale_kernel, groups, dp, cap, columns * dp),
        in_specs=[VMEM],
        out_specs=VMEM,
        out_shape=jax.ShapeDtypeStruct((groups * 8, 128), F32),
        compiler_params=small,
        cost_estimate=pl.CostEstimate(flops=0, bytes_accessed=4 * weight.size, transcendentals=0),
        name="scale",
    )(squares)
    even = [parts[0]] + [across(parts[j], 2 * j) for j in range(1, pairs)]
    *even, scales = lax.optimization_barrier((*even, scales))
    arrived = jax.ShapeDtypeStruct((pairs * cap * size, columns), BF16)
    odd = pl.pallas_call(
        pack_kernel, in_specs=[VMEM] * pairs, out_specs=VMEM, out_shape=arrived, compiler_params=small, name="pack"
    )(*even)
    odd = across(odd, 1)
    gain = out_gain[None, :]
    base, order = pl.pallas_call(
        functools.partial(base_kernel, groups, cap, size),
        in_specs=[VMEM] * (3 + pairs),
        out_specs=[VMEM] * 2,
        out_shape=[
            jax.ShapeDtypeStruct(text.shape, BF16),
            jax.ShapeDtypeStruct((seq_len, pairs * cap * size), BF16),
        ],
        scratch_shapes=[pltpu.VMEM(arrived.shape, BF16)],
        compiler_params=small,
        cost_estimate=pl.CostEstimate(flops=0, bytes_accessed=2 * weight.size, transcendentals=0),
        name="base",
    )(scales, gain, text, *even)
    return pl.pallas_call(
        functools.partial(place_kernel, groups, cap, size),
        in_specs=[VMEM] * 5,
        out_specs=VMEM,
        out_shape=jax.ShapeDtypeStruct(text.shape, BF16),
        scratch_shapes=[pltpu.VMEM(arrived.shape, BF16)],
        compiler_params=small,
        name="place",
    )(scales, gain, odd, base, order)


def general(
    vis_features, vis_gain, proj_weight, proj_bias, text_embed, out_gain, image_counts, owner_block, offsets
):
    groups = lax.axis_size("grp")
    width = proj_weight.shape[1] * lax.axis_size("dp")
    slots_device = owner_block.shape[0]
    per_image = vis_features.shape[0] // slots_device
    columns = proj_weight.shape[1]
    seq_len = text_embed.shape[0]
    capacity = seq_len // (groups * per_image)
    features_f = vis_features.astype(jnp.float32)
    normed = (
        features_f
        * lax.rsqrt(jnp.mean(features_f * features_f, axis=-1, keepdims=True) + EPS_VIS)
        * vis_gain
    ).astype(jnp.bfloat16)
    slot_local = jnp.arange(slots_device, dtype=jnp.int32)
    live_offsets = jnp.where(slot_local < image_counts[0], offsets, -1)
    block_owner, block_offsets = (
        lax.all_gather(owner_block, "dp", axis=0, tiled=True),
        lax.all_gather(live_offsets, "dp", axis=0, tiled=True),
    )
    projected = (
        jnp.dot(
            lax.all_gather(normed, "dp", axis=0, tiled=True),
            proj_weight,
            preferred_element_type=jnp.float32,
        )
        + proj_bias
    ).astype(jnp.bfloat16)
    block_slots = block_owner.shape[0]
    earlier = jnp.arange(block_slots)[:, None] > jnp.arange(block_slots)[None, :]
    same_owner = block_owner[:, None] == block_owner[None, :]
    rank_in = jnp.sum(same_owner & earlier, axis=1)
    bucket = block_owner * capacity + rank_in
    selector = jnp.arange(groups * capacity, dtype=jnp.int32)[:, None] == bucket[None, :]
    flat_rows = projected.reshape(block_slots, per_image * columns)
    bucketed = jnp.dot(
        selector.astype(jnp.bfloat16), flat_rows, preferred_element_type=jnp.float32
    ).astype(jnp.bfloat16)
    bucketed = bucketed.reshape(groups, capacity * per_image * columns)
    bucket_offsets = jnp.max(jnp.where(selector, block_offsets[None, :], -1), axis=1).reshape(
        groups, capacity
    )
    arrived, arrived_offsets = (
        lax.all_to_all(bucketed, "grp", split_axis=0, concat_axis=0, tiled=True),
        lax.all_to_all(bucket_offsets, "grp", split_axis=0, concat_axis=0, tiled=True),
    )
    received = arrived.reshape(groups * capacity * per_image, columns)
    starts = arrived_offsets.reshape(groups * capacity)
    target = jnp.where(
        starts[:, None] >= 0,
        starts[:, None] + jnp.arange(per_image, dtype=jnp.int32)[None, :],
        seq_len,
    )
    target = target.reshape(-1).astype(jnp.int32)
    merged = text_embed.at[target].set(received, mode="drop")
    local_squares = jnp.sum(jnp.square(merged.astype(jnp.float32)), axis=1)
    row_total = lax.psum(local_squares, "dp")
    inverse_rms = lax.rsqrt(row_total / width + EPS_OUT)
    hidden = merged.astype(jnp.float32) * inverse_rms[:, None] * out_gain
    return hidden.astype(jnp.bfloat16)


def on_device(vis, vis_gain, weight, bias, text, out_gain, counts, owners, offsets):
    groups, dp = lax.axis_size("grp"), lax.axis_size("dp")
    per_image = vis.shape[0] // owners.shape[0]
    cap = text.shape[0] // (groups * per_image)
    full = dp * owners.shape[0] == groups * cap and groups * cap * per_image == text.shape[0]
    fits = dp == 4 and groups & (groups - 1) == 0 and per_image == 16 and cap == 2 and text.shape[0] <= 512
    fits = fits and owners.shape[0] % 4 == 0 and weight.shape[1] % 1024 == 0
    form = fast if full and fits else general
    return form(vis, vis_gain, weight, bias, text, out_gain, counts, owners, offsets)


def solution(mesh):
    return jax.shard_map(
        on_device,
        mesh=mesh,
        in_specs=(
            P(("grp", "dp"), None),
            P(),
            P(None, "dp"),
            P("dp"),
            P("grp", "dp"),
            P("dp"),
            P(("grp", "dp")),
            P(("grp", "dp")),
            P(("grp", "dp")),
        ),
        out_specs=P("grp", "dp"),
        check_vma=False,
    )
```

```python
import functools

import jax
import jax.numpy as jnp
from jax import lax
from jax.experimental import pallas as pl
from jax.experimental.pallas import tpu as pltpu
from jax.sharding import PartitionSpec as P

EPS_VIS = 1e-06
EPS_OUT = 1e-05
TILE = (8, 128)
F32 = jnp.float32
BF16 = jnp.bfloat16
VMEM = pl.BlockSpec(memory_space=pltpu.VMEM)
SMEM = pl.BlockSpec(memory_space=pltpu.SMEM)
ANY = pl.BlockSpec(memory_space=pl.ANY)
LIMIT = 16 << 20


def lanes():
    return lax.broadcasted_iota(jnp.int32, TILE, 1)


def tables_kernel(slots, size, text, vis, owners, offsets, counts, squares, info, own):
    lane = lanes()
    tile = jnp.zeros(TILE, F32)
    for c in range(text.shape[0] // 16):
        x = text[c * 16 : (c + 1) * 16, :].astype(F32)
        sums = jnp.sum(x * x, axis=1, keepdims=True)
        tile = jnp.where(lane == 2 * c, sums[:8], tile)
        tile = jnp.where(lane == 2 * c + 1, sums[8:], tile)
    squares[...] = tile
    row = lax.axis_index("dp")
    lane = lax.broadcasted_iota(jnp.int32, (size, 128), 1)
    for i in range(slots):
        code = jnp.where(i < counts[0], offsets[i] // size + 1, 0)
        known = jnp.where(lane == 0, owners[i], jnp.where(lane == 1, row * slots + i, jnp.where(lane == 2, code, 0)))
        info[i * size : (i + 1) * size, :] = known.astype(F32).astype(BF16)
    own[...] = vis[...]


def pass_kernel(own, inner, gain, sent, later):
    row = lax.axis_index("dp")
    depth, stretch = inner.shape[1], sent.shape[1]
    rows = jnp.where(jnp.logical_or(row == 1, row == 2), inner[...], own[...])
    rows = normed(rows, gain[...].reshape(1, depth))
    sent[...] = rows[:, :stretch]
    later[...] = rows[:, stretch:]


def hold_kernel(weight, tile, out):
    del weight
    out[...] = tile[...]


def normed(rows, gain):
    x = rows.astype(F32)
    scale = lax.rsqrt(jnp.mean(x * x, axis=-1, keepdims=True) + EPS_VIS)
    return (x * scale * gain).astype(BF16)


def early_kernel(own, outer, inner, ends, gain, weight, bias, y, x):
    row = lax.axis_index("dp")
    middle = jnp.logical_or(row == 1, row == 2)
    depth, columns = weight.shape
    count = own.shape[0]
    g = gain[...].reshape(1, depth)
    x[0:count] = normed(own[...], g)
    x[count : 2 * count] = normed(outer[...], g)
    x[2 * count : 3 * count] = normed(jnp.where(middle, inner[...], ends[...]), g)
    block = 256
    for n in range(columns // block):
        at = slice(n * block, (n + 1) * block)
        y[:, at] = (jnp.dot(x[...], weight[:, at], preferred_element_type=F32) + bias[:, at]).astype(BF16)


def late_kernel(last, weight, bias, total):
    depth = last.shape[1]
    total[...] = jnp.dot(last[...], weight[:depth, :], preferred_element_type=F32) + bias[...]


def project_kernel(groups, cap, size, i3, i2, i1, i0, last, weight, total, early, text_squares, *rest):
    *parts, tiles, y, z, codes = rest
    me = lax.axis_index("grp")
    depth, columns = weight.shape
    stretch = last.shape[1]
    down = jnp.concatenate([i0[...], i1[...], i2[...], i3[...]], axis=0).astype(F32)
    rows = down.shape[0]
    across = down.T
    owner_down, slot_down = down[:, 0:1], down[:, 1:2]
    owner, slot = across[0:1, :], across[1:2, :]
    earlier = jnp.logical_and(owner_down == owner, slot_down < slot)
    rank = jnp.sum(earlier.astype(F32), axis=0, keepdims=True).astype(jnp.int32) // size
    place = owner.astype(jnp.int32) ^ me
    position = lax.broadcasted_iota(jnp.int32, (1, rows), 1) % size
    seat = (place * cap + rank) * size + position
    first = position == 0
    image = lax.broadcasted_iota(jnp.int32, (1, rows), 1) // size
    at = [
        pl.multiple_of(jnp.sum(jnp.where(jnp.logical_and(first, image == i), seat, 0)), size)
        for i in range(rows // size)
    ]
    block = 256
    for n in range(columns // block):
        part = slice(n * block, (n + 1) * block)
        more = jnp.dot(last[...], weight[depth - stretch :, part], preferred_element_type=F32)
        z[:, part] = (total[:, part] + more).astype(BF16)
    count = early.shape[0] // size
    for i in range(rows // size):
        source, n = (early, i) if i < count else (z, i - count)
        y[pl.ds(at[i], size), :] = source[n * size : (n + 1) * size]
        codes[pl.ds(at[i], size), :] = down[i * size : (i + 1) * size]
    chunk = rows // len(parts)
    for m, part in enumerate(parts):
        part[...] = y[m * chunk : (m + 1) * chunk]
    lane = lanes()
    copies = tiles.shape[0] // (8 * groups)
    for k in range(groups):
        tile = jnp.zeros(TILE, F32)
        for r in range(cap):
            start = (k * cap + r) * size
            wide = y[start : start + size, :].astype(F32)
            tile = jnp.where(lane == 2 * cap + r, codes[start : start + 8, 2:3], tile)
            sums = jnp.sum(wide * wide, axis=1, keepdims=True)
            tile = jnp.where(lane == 2 * r, sums[:8], jnp.where(lane == 2 * r + 1, sums[8:], tile))
        if k == 0:
            tile = jnp.where(lane < 3 * cap, tile, pltpu.roll(text_squares[...], 3 * cap, 1))
        for q in range(copies):
            tiles[pl.ds(pl.multiple_of(((me ^ k) * copies + q) * 8, 8), 8), :] = tile


def scale_kernel(groups, dp, cap, width, squares, scales):
    me = lax.axis_index("grp")
    lane = lanes()
    is_code = jnp.logical_and(lane >= 2 * cap, lane < 3 * cap)
    for k in range(groups):
        base = (me ^ k) * (dp * 8)
        tile = squares[pl.ds(pl.multiple_of(base, 8), 8), :]
        code = tile
        for d in range(1, dp):
            tile = tile + squares[pl.ds(pl.multiple_of(base + d * 8, 8), 8), :]
        scales[k * 8 : (k + 1) * 8, :] = jnp.where(is_code, code, lax.rsqrt(tile / width + EPS_OUT))


def pack_kernel(*refs):
    *parts, out = refs
    rows = parts[0].shape[0] // 2
    for n, part in enumerate(parts):
        out[n * rows : (n + 1) * rows, :] = part[rows:, :]


def scaled(cap, size, k, rows, scales, gain):
    scale = scales[k * 8 : (k + 1) * 8, :]
    out = []
    for r in range(cap):
        inverse = jnp.concatenate([scale[:, 2 * r : 2 * r + 1], scale[:, 2 * r + 1 : 2 * r + 2]], axis=0)
        out.append((rows[r * size : (r + 1) * size, :].astype(F32) * inverse * gain).astype(BF16))
    return out


def moves(seq_len, cap, size, senders, scales):
    lane = 2 * cap
    codes = [
        jnp.broadcast_to(scales[k * 8 : (k + 1) * 8, lane + r : lane + r + 1], TILE)
        for k in senders
        for r in range(cap)
        for _ in range(size // 8)
    ]
    code = jnp.concatenate(codes, axis=0).T[0:1, :].astype(jnp.int32)
    position = lax.broadcasted_iota(jnp.int32, code.shape, 1) % size
    target = jnp.where(code > 0, (code - 1) * size + position, -1)
    return (lax.broadcasted_iota(jnp.int32, (seq_len, code.shape[1]), 0) == target).astype(F32)


def base_kernel(groups, cap, size, scales, gain, text, *rest):
    *even, base, order_odd, rows = rest
    seq_len = text.shape[0]
    g = gain[...]
    order = moves(seq_len, cap, size, range(0, groups, 2), scales)
    odd = moves(seq_len, cap, size, range(1, groups, 2), scales)
    order_odd[...] = odd.astype(BF16)
    covered = jnp.sum(order + odd, axis=1, keepdims=True)
    for n, part in enumerate(even):
        for r, x in enumerate(scaled(cap, size, 2 * n, part, scales, g)):
            at = (n * cap + r) * size
            rows[at : at + size, :] = x
    moved = jnp.dot(order.astype(BF16), rows[...], preferred_element_type=F32)
    own = scales[0:8, :]
    for c in range(seq_len // 16):
        at = 3 * cap + 2 * c
        inverse = jnp.concatenate([own[:, at : at + 1], own[:, at + 1 : at + 2]], axis=0)
        part = slice(c * 16, (c + 1) * 16)
        x = text[part, :].astype(F32) * inverse * g
        base[part, :] = jnp.where(covered[part] > 0, moved[part], x).astype(BF16)


def place_kernel(groups, cap, size, scales, gain, odd, base, order, out, rows, done, sems):
    columns = out.shape[1]
    block = columns // sems.shape[0]
    copies = []
    for c in range(sems.shape[0]):
        part = slice(c * block, (c + 1) * block)
        g = gain[:, part]
        for n, k in enumerate(range(1, groups, 2)):
            at = n * cap * size
            for r, x in enumerate(scaled(cap, size, k, odd[at : at + cap * size, part], scales, g)):
                rows[at + r * size : at + (r + 1) * size, part] = x
        moved = jnp.dot(order[...], rows[:, part], preferred_element_type=F32)
        done[:, part] = (base[:, part].astype(F32) + moved).astype(BF16)
        copies.append(pltpu.make_async_copy(done.at[:, part], out.at[:, part], sems.at[c]))
        copies[-1].start()
    for copy in copies:
        copy.wait()


def outer(x):
    return lax.ppermute(x, "dp", [(0, 1), (1, 0), (2, 3), (3, 2)])


def inner(x):
    return lax.ppermute(x, "dp", [(1, 2), (2, 1), (0, 0), (3, 3)])


def ends(x):
    return lax.ppermute(x, "dp", [(0, 3), (3, 0), (1, 1), (2, 2)])


def mirror(x):
    return lax.ppermute(x, "dp", [(0, 3), (1, 2), (2, 1), (3, 0)])


def second(x):
    return lax.ppermute(x, "dp", [(0, 2), (1, 3), (2, 0), (3, 1)])


def far(x):
    return lax.ppermute(x, "dp", [(0, 2), (1, 0), (2, 3), (3, 1)])


def across(x, k):
    return lax.ppermute(x, "grp", [(i, i ^ k) for i in range(lax.axis_size("grp"))])


def fast(vis, vis_gain, weight, bias, text, out_gain, counts, owners, offsets):
    groups, dp = lax.axis_size("grp"), lax.axis_size("dp")
    devices = groups * dp
    slots = owners.shape[0]
    size = vis.shape[0] // slots
    seq_len, columns = text.shape
    cap = seq_len // (groups * size)
    depth = vis.shape[1]
    small = pltpu.CompilerParams(vmem_limit_bytes=LIMIT)
    count = slots * size
    tile = jax.ShapeDtypeStruct(TILE, F32)
    bias = bias[None, :]

    x_inner, x_outer = inner(vis), outer(vis)
    text_squares, info, own = pl.pallas_call(
        functools.partial(tables_kernel, slots, size),
        in_specs=[VMEM, VMEM, SMEM, SMEM, SMEM],
        out_specs=[VMEM] * 3,
        out_shape=[tile, jax.ShapeDtypeStruct((count, 128), BF16), jax.ShapeDtypeStruct(vis.shape, BF16)],
        compiler_params=small,
        name="tables",
    )(text, vis, owners, offsets, counts)
    x_ends = ends(vis)
    weight = pltpu.with_memory_space_constraint(weight, pltpu.VMEM)
    text_squares = pl.pallas_call(
        hold_kernel,
        in_specs=[ANY, VMEM],
        out_specs=VMEM,
        out_shape=tile,
        compiler_params=small,
        cost_estimate=pl.CostEstimate(flops=0, bytes_accessed=2 * weight.size, transcendentals=0),
        name="hold",
    )(weight, text_squares)
    x_inner, text_squares = lax.optimization_barrier((x_inner, text_squares))
    stretches = depth // 3 // 128 * 128
    stretches = (depth - stretches, stretches)
    stretch = depth // 3 // 128 * 128
    sent, later = pl.pallas_call(
        pass_kernel,
        in_specs=[VMEM] * 3,
        out_specs=[VMEM] * 2,
        out_shape=[jax.ShapeDtypeStruct((count, n), BF16) for n in (depth - stretch, stretch)],
        compiler_params=small,
        name="pass",
    )(own, x_inner, vis_gain)
    sent, later, x_outer = lax.optimization_barrier((sent, later, x_outer))
    last_a = far(sent)
    known = (second(info), mirror(info), outer(info), info)
    last_b = far(later)
    cost = pl.CostEstimate(
        flops=2 * 3 * count * depth * columns, bytes_accessed=2 * weight.size, transcendentals=0
    )
    early = pl.pallas_call(
        early_kernel,
        in_specs=[VMEM] * 7,
        out_specs=VMEM,
        out_shape=jax.ShapeDtypeStruct((3 * count, columns), BF16),
        scratch_shapes=[pltpu.VMEM((3 * count, depth), BF16)],
        compiler_params=small,
        cost_estimate=pl.CostEstimate(flops=0, bytes_accessed=0, transcendentals=0),
        name="early",
    )(own, x_outer, x_inner, x_ends, vis_gain, weight, bias)
    pairs = groups // 2
    total = pl.pallas_call(
        late_kernel,
        in_specs=[VMEM] * 3,
        out_specs=VMEM,
        out_shape=jax.ShapeDtypeStruct((count, columns), F32),
        compiler_params=small,
        cost_estimate=pl.CostEstimate(flops=0, bytes_accessed=0, transcendentals=0),
        name="late",
    )(last_a, weight, bias)
    *parts, squares = pl.pallas_call(
        functools.partial(project_kernel, groups, cap, size),
        in_specs=[VMEM] * 9,
        out_specs=[VMEM] * (pairs + 1),
        out_shape=[jax.ShapeDtypeStruct((2 * cap * size, columns), BF16)] * pairs
        + [jax.ShapeDtypeStruct((devices * 8, 128), F32)],
        scratch_shapes=[
            pltpu.VMEM((dp * count, columns), BF16),
            pltpu.VMEM((count, columns), BF16),
            pltpu.VMEM((dp * count, 128), F32),
        ],
        compiler_params=small,
        cost_estimate=cost,
        name="project",
    )(*known, last_b, weight, total, early, text_squares)
    squares = lax.all_to_all(squares, ("grp", "dp"), 0, 0, tiled=True)
    scales = pl.pallas_call(
        functools.partial(scale_kernel, groups, dp, cap, columns * dp),
        in_specs=[VMEM],
        out_specs=VMEM,
        out_shape=jax.ShapeDtypeStruct((groups * 8, 128), F32),
        compiler_params=small,
        cost_estimate=pl.CostEstimate(flops=0, bytes_accessed=4 * weight.size, transcendentals=0),
        name="scale",
    )(squares)
    even = [parts[0]] + [across(parts[j], 2 * j) for j in range(1, pairs)]
    *even, scales = lax.optimization_barrier((*even, scales))
    arrived = jax.ShapeDtypeStruct((pairs * cap * size, columns), BF16)
    odd = pl.pallas_call(
        pack_kernel, in_specs=[VMEM] * pairs, out_specs=VMEM, out_shape=arrived, compiler_params=small, name="pack"
    )(*even)
    odd = across(odd, 1)
    gain = out_gain[None, :]
    base, order = pl.pallas_call(
        functools.partial(base_kernel, groups, cap, size),
        in_specs=[VMEM] * (3 + pairs),
        out_specs=[VMEM] * 2,
        out_shape=[
            jax.ShapeDtypeStruct(text.shape, BF16),
            jax.ShapeDtypeStruct((seq_len, pairs * cap * size), BF16),
        ],
        scratch_shapes=[pltpu.VMEM(arrived.shape, BF16)],
        compiler_params=small,
        cost_estimate=pl.CostEstimate(flops=0, bytes_accessed=2 * weight.size, transcendentals=0),
        name="base",
    )(scales, gain, text, *even)
    return pl.pallas_call(
        functools.partial(place_kernel, groups, cap, size),
        in_specs=[VMEM] * 5,
        out_specs=ANY,
        out_shape=jax.ShapeDtypeStruct(text.shape, BF16),
        scratch_shapes=[
            pltpu.VMEM(arrived.shape, BF16),
            pltpu.VMEM(text.shape, BF16),
            pltpu.SemaphoreType.DMA((4,)),
        ],
        compiler_params=small,
        name="place",
    )(scales, gain, odd, base, order)


def general(
    vis_features, vis_gain, proj_weight, proj_bias, text_embed, out_gain, image_counts, owner_block, offsets
):
    groups = lax.axis_size("grp")
    width = proj_weight.shape[1] * lax.axis_size("dp")
    slots_device = owner_block.shape[0]
    per_image = vis_features.shape[0] // slots_device
    columns = proj_weight.shape[1]
    seq_len = text_embed.shape[0]
    capacity = seq_len // (groups * per_image)
    features_f = vis_features.astype(jnp.float32)
    normed = (
        features_f
        * lax.rsqrt(jnp.mean(features_f * features_f, axis=-1, keepdims=True) + EPS_VIS)
        * vis_gain
    ).astype(jnp.bfloat16)
    slot_local = jnp.arange(slots_device, dtype=jnp.int32)
    live_offsets = jnp.where(slot_local < image_counts[0], offsets, -1)
    block_owner, block_offsets = (
        lax.all_gather(owner_block, "dp", axis=0, tiled=True),
        lax.all_gather(live_offsets, "dp", axis=0, tiled=True),
    )
    projected = (
        jnp.dot(
            lax.all_gather(normed, "dp", axis=0, tiled=True),
            proj_weight,
            preferred_element_type=jnp.float32,
        )
        + proj_bias
    ).astype(jnp.bfloat16)
    block_slots = block_owner.shape[0]
    earlier = jnp.arange(block_slots)[:, None] > jnp.arange(block_slots)[None, :]
    same_owner = block_owner[:, None] == block_owner[None, :]
    rank_in = jnp.sum(same_owner & earlier, axis=1)
    bucket = block_owner * capacity + rank_in
    selector = jnp.arange(groups * capacity, dtype=jnp.int32)[:, None] == bucket[None, :]
    flat_rows = projected.reshape(block_slots, per_image * columns)
    bucketed = jnp.dot(
        selector.astype(jnp.bfloat16), flat_rows, preferred_element_type=jnp.float32
    ).astype(jnp.bfloat16)
    bucketed = bucketed.reshape(groups, capacity * per_image * columns)
    bucket_offsets = jnp.max(jnp.where(selector, block_offsets[None, :], -1), axis=1).reshape(
        groups, capacity
    )
    arrived, arrived_offsets = (
        lax.all_to_all(bucketed, "grp", split_axis=0, concat_axis=0, tiled=True),
        lax.all_to_all(bucket_offsets, "grp", split_axis=0, concat_axis=0, tiled=True),
    )
    received = arrived.reshape(groups * capacity * per_image, columns)
    starts = arrived_offsets.reshape(groups * capacity)
    target = jnp.where(
        starts[:, None] >= 0,
        starts[:, None] + jnp.arange(per_image, dtype=jnp.int32)[None, :],
        seq_len,
    )
    target = target.reshape(-1).astype(jnp.int32)
    merged = text_embed.at[target].set(received, mode="drop")
    local_squares = jnp.sum(jnp.square(merged.astype(jnp.float32)), axis=1)
    row_total = lax.psum(local_squares, "dp")
    inverse_rms = lax.rsqrt(row_total / width + EPS_OUT)
    hidden = merged.astype(jnp.float32) * inverse_rms[:, None] * out_gain
    return hidden.astype(jnp.bfloat16)


def on_device(vis, vis_gain, weight, bias, text, out_gain, counts, owners, offsets):
    groups, dp = lax.axis_size("grp"), lax.axis_size("dp")
    per_image = vis.shape[0] // owners.shape[0]
    cap = text.shape[0] // (groups * per_image)
    full = dp * owners.shape[0] == groups * cap and groups * cap * per_image == text.shape[0]
    fits = dp == 4 and groups & (groups - 1) == 0 and per_image == 16 and cap == 2 and text.shape[0] <= 512
    fits = fits and owners.shape[0] % 4 == 0 and weight.shape[1] % 1024 == 0
    form = fast if full and fits else general
    return form(vis, vis_gain, weight, bias, text, out_gain, counts, owners, offsets)


def solution(mesh):
    return jax.shard_map(
        on_device,
        mesh=mesh,
        in_specs=(
            P(("grp", "dp"), None),
            P(),
            P(None, "dp"),
            P("dp"),
            P("grp", "dp"),
            P("dp"),
            P(("grp", "dp")),
            P(("grp", "dp")),
            P(("grp", "dp")),
        ),
        out_specs=P("grp", "dp"),
        check_vma=False,
    )
```

```python
import functools

import jax
import jax.numpy as jnp
from jax import lax
from jax.experimental import pallas as pl
from jax.experimental.pallas import tpu as pltpu
from jax.sharding import PartitionSpec as P

EPS_VIS = 1e-06
EPS_OUT = 1e-05
TILE = (8, 128)
TEXT = 64
F32 = jnp.float32
BF16 = jnp.bfloat16
VMEM = pl.BlockSpec(memory_space=pltpu.VMEM)
SMEM = pl.BlockSpec(memory_space=pltpu.SMEM)
ANY = pl.BlockSpec(memory_space=pl.ANY)
LIMIT = 16 << 20


def lanes():
    return lax.broadcasted_iota(jnp.int32, TILE, 1)


def tables_kernel(slots, size, text, vis, owners, offsets, counts, info, own, squares):
    lane = lanes()
    tile = jnp.zeros(TILE, F32)
    for c in range(text.shape[0] // 16):
        x = text[c * 16 : (c + 1) * 16, :].astype(F32)
        sums = jnp.sum(x * x, axis=1, keepdims=True)
        tile = jnp.where(lane == 2 * c, sums[:8], tile)
        tile = jnp.where(lane == 2 * c + 1, sums[8:], tile)
    squares[...] = tile
    row = lax.axis_index("dp")
    known = jnp.zeros(TILE, jnp.int32)
    for i in range(slots):
        code = jnp.where(i < counts[0], offsets[i] // size + 1, 0)
        for n, value in enumerate((owners[i], row * slots + i, code)):
            known = jnp.where(lane == n * slots + i, value, known)
    info[...] = known.astype(F32) + pltpu.roll(tile, TEXT, 1)
    own[...] = vis[...]


def spread(slots, size, tiles):
    lane = lax.broadcasted_iota(jnp.int32, (size, 128), 1)
    rows = []
    for tile in tiles:
        for i in range(slots):
            owner, slot, code = [tile[0:1, n * slots + i : n * slots + i + 1] for n in range(3)]
            rows.append(jnp.where(lane == 0, owner, jnp.where(lane == 1, slot, jnp.where(lane == 2, code, 0))))
    return jnp.concatenate(rows, axis=0)


def pass_kernel(own, inner, gain, sent, later):
    row = lax.axis_index("dp")
    depth, stretch = inner.shape[1], sent.shape[1]
    rows = jnp.where(jnp.logical_or(row == 1, row == 2), inner[...], own[...])
    rows = normed(rows, gain[...].reshape(1, depth))
    sent[...] = rows[:, :stretch]
    later[...] = rows[:, stretch:]


def hold_kernel(weight, tile, out):
    del weight
    out[...] = tile[...]


def normed(rows, gain):
    x = rows.astype(F32)
    scale = lax.rsqrt(jnp.mean(x * x, axis=-1, keepdims=True) + EPS_VIS)
    return (x * scale * gain).astype(BF16)


def early_kernel(own, outer, inner, ends, gain, weight, bias, y, x):
    row = lax.axis_index("dp")
    middle = jnp.logical_or(row == 1, row == 2)
    depth, columns = weight.shape
    count = own.shape[0]
    g = gain[...].reshape(1, depth)
    x[0:count] = normed(own[...], g)
    x[count : 2 * count] = normed(outer[...], g)
    x[2 * count : 3 * count] = normed(jnp.where(middle, inner[...], ends[...]), g)
    block = 256
    for n in range(columns // block):
        at = slice(n * block, (n + 1) * block)
        y[:, at] = (jnp.dot(x[...], weight[:, at], preferred_element_type=F32) + bias[:, at]).astype(BF16)


def late_kernel(last, weight, bias, total):
    depth = last.shape[1]
    total[...] = jnp.dot(last[...], weight[:depth, :], preferred_element_type=F32) + bias[...]


def project_kernel(groups, cap, size, width, i3, i2, i1, i0, last, weight, total, early, text, *rest):
    *parts, tiles, text_scale, y, z, codes = rest
    me = lax.axis_index("grp")
    depth, columns = weight.shape
    stretch = last.shape[1]
    down = spread(last.shape[0] // size, size, [i0[...], i1[...], i2[...], i3[...]])
    rows = down.shape[0]
    across = down.T
    owner_down, slot_down = down[:, 0:1], down[:, 1:2]
    owner, slot = across[0:1, :], across[1:2, :]
    earlier = jnp.logical_and(owner_down == owner, slot_down < slot)
    rank = jnp.sum(earlier.astype(F32), axis=0, keepdims=True).astype(jnp.int32) // size
    place = owner.astype(jnp.int32) ^ me
    position = lax.broadcasted_iota(jnp.int32, (1, rows), 1) % size
    seat = (place * cap + rank) * size + position
    first = position == 0
    image = lax.broadcasted_iota(jnp.int32, (1, rows), 1) // size
    at = [
        pl.multiple_of(jnp.sum(jnp.where(jnp.logical_and(first, image == i), seat, 0)), size)
        for i in range(rows // size)
    ]
    block = 256
    for n in range(columns // block):
        part = slice(n * block, (n + 1) * block)
        more = jnp.dot(last[...], weight[depth - stretch :, part], preferred_element_type=F32)
        z[:, part] = (total[:, part] + more).astype(BF16)
    count = early.shape[0] // size
    for i in range(rows // size):
        source, n = (early, i) if i < count else (z, i - count)
        y[pl.ds(at[i], size), :] = source[n * size : (n + 1) * size]
        codes[pl.ds(at[i], size), :] = down[i * size : (i + 1) * size]
    chunk = rows // len(parts)
    for m, part in enumerate(parts):
        part[...] = y[m * chunk : (m + 1) * chunk]
    lane = lanes()
    others = pltpu.roll(i1[...] + i2[...] + i3[...], 128 - TEXT, 1)
    text_scale[...] = lax.rsqrt((text[...] + others) / width + EPS_OUT)
    columns = []
    for k in range(groups):
        wide = y[k * cap * size : (k + 1) * cap * size, :].astype(F32)
        sums = jnp.sum(wide * wide, axis=1, keepdims=True)
        code = [codes[(k * cap + r) * size : (k * cap + r) * size + 1, 2:3] for r in range(cap)]
        fill = jnp.zeros((128 - cap * size - cap, 1), F32)
        columns.append(jnp.concatenate([sums, *code, fill], axis=0))
    lane = lax.broadcasted_iota(jnp.int32, (128, 128), 1)
    told = jnp.zeros((128, 128), F32)
    for k in range(groups):
        told = jnp.where(lane == k, columns[k], told)
    told = told.T
    copies = tiles.shape[0] // groups
    for k in range(groups):
        for q in range(copies):
            tiles[pl.ds((me ^ k) * copies + q, 1), :] = told[k : k + 1, :]


def scale_kernel(groups, dp, rows, width, squares, scales):
    me = lax.axis_index("grp")
    source = lax.broadcasted_iota(jnp.int32, squares.shape, 0)
    lane = lax.broadcasted_iota(jnp.int32, (1, 128), 1)
    told = []
    for k in range(groups):
        mine = source // dp == (me ^ k)
        total = jnp.sum(jnp.where(mine, squares[...], 0), axis=0, keepdims=True)
        code = jnp.sum(jnp.where(source == (me ^ k) * dp, squares[...], 0), axis=0, keepdims=True)
        told.append(jnp.where(lane < rows, lax.rsqrt(total / width + EPS_OUT), code))
    told.append(jnp.zeros((128 - groups, 128), F32))
    scales[...] = jnp.concatenate(told, axis=0).T


def pack_kernel(*refs):
    *parts, out = refs
    rows = parts[0].shape[0] // 2
    for n, part in enumerate(parts):
        out[n * rows : (n + 1) * rows, :] = part[rows:, :]


def scaled(cap, size, k, rows, scales, gain):
    out = []
    for r in range(cap):
        inverse = scales[r * size : (r + 1) * size, k : k + 1]
        out.append((rows[r * size : (r + 1) * size, :].astype(F32) * inverse * gain).astype(BF16))
    return out


def moves(seq_len, cap, size, senders, scales):
    at = cap * size
    codes = [
        jnp.broadcast_to(scales[at + r : at + r + 1, k : k + 1], TILE)
        for k in senders
        for r in range(cap)
        for _ in range(size // 8)
    ]
    code = jnp.concatenate(codes, axis=0).T[0:1, :].astype(jnp.int32)
    position = lax.broadcasted_iota(jnp.int32, code.shape, 1) % size
    target = jnp.where(code > 0, (code - 1) * size + position, -1)
    return (lax.broadcasted_iota(jnp.int32, (seq_len, code.shape[1]), 0) == target).astype(F32)


def base_kernel(groups, cap, size, scales, text_scale, gain, text, *rest):
    *even, base, order_odd, rows = rest
    seq_len = text.shape[0]
    g = gain[...]
    order = moves(seq_len, cap, size, range(0, groups, 2), scales)
    odd = moves(seq_len, cap, size, range(1, groups, 2), scales)
    order_odd[...] = odd.astype(BF16)
    covered = jnp.sum(order + odd, axis=1, keepdims=True)
    for n, part in enumerate(even):
        for r, x in enumerate(scaled(cap, size, 2 * n, part, scales, g)):
            at = (n * cap + r) * size
            rows[at : at + size, :] = x
    moved = jnp.dot(order.astype(BF16), rows[...], preferred_element_type=F32)
    for c in range(seq_len // 16):
        inverse = jnp.concatenate([text_scale[:, 2 * c : 2 * c + 1], text_scale[:, 2 * c + 1 : 2 * c + 2]], axis=0)
        part = slice(c * 16, (c + 1) * 16)
        x = text[part, :].astype(F32) * inverse * g
        base[part, :] = jnp.where(covered[part] > 0, moved[part], x).astype(BF16)


def place_kernel(groups, cap, size, scales, gain, odd, base, order, out, rows, done, sems):
    columns = out.shape[1]
    block = columns // sems.shape[0]
    copies = []
    for c in range(sems.shape[0]):
        part = slice(c * block, (c + 1) * block)
        g = gain[:, part]
        for n, k in enumerate(range(1, groups, 2)):
            at = n * cap * size
            for r, x in enumerate(scaled(cap, size, k, odd[at : at + cap * size, part], scales, g)):
                rows[at + r * size : at + (r + 1) * size, part] = x
        moved = jnp.dot(order[...], rows[:, part], preferred_element_type=F32)
        done[:, part] = (base[:, part].astype(F32) + moved).astype(BF16)
        copies.append(pltpu.make_async_copy(done.at[:, part], out.at[:, part], sems.at[c]))
        copies[-1].start()
    for copy in copies:
        copy.wait()


def outer(x):
    return lax.ppermute(x, "dp", [(0, 1), (1, 0), (2, 3), (3, 2)])


def inner(x):
    return lax.ppermute(x, "dp", [(1, 2), (2, 1), (0, 0), (3, 3)])


def ends(x):
    return lax.ppermute(x, "dp", [(0, 3), (3, 0), (1, 1), (2, 2)])


def mirror(x):
    return lax.ppermute(x, "dp", [(0, 3), (1, 2), (2, 1), (3, 0)])


def second(x):
    return lax.ppermute(x, "dp", [(0, 2), (1, 3), (2, 0), (3, 1)])


def far(x):
    return lax.ppermute(x, "dp", [(0, 2), (1, 0), (2, 3), (3, 1)])


def across(x, k):
    return lax.ppermute(x, "grp", [(i, i ^ k) for i in range(lax.axis_size("grp"))])


def fast(vis, vis_gain, weight, bias, text, out_gain, counts, owners, offsets):
    groups, dp = lax.axis_size("grp"), lax.axis_size("dp")
    devices = groups * dp
    slots = owners.shape[0]
    size = vis.shape[0] // slots
    seq_len, columns = text.shape
    cap = seq_len // (groups * size)
    depth = vis.shape[1]
    small = pltpu.CompilerParams(vmem_limit_bytes=LIMIT)
    count = slots * size
    tile = jax.ShapeDtypeStruct(TILE, F32)
    bias = bias[None, :]

    x_inner, x_outer = inner(vis), outer(vis)
    info, own, held = pl.pallas_call(
        functools.partial(tables_kernel, slots, size),
        in_specs=[VMEM, VMEM, SMEM, SMEM, SMEM],
        out_specs=[VMEM] * 3,
        out_shape=[tile, jax.ShapeDtypeStruct(vis.shape, BF16), tile],
        compiler_params=small,
        name="tables",
    )(text, vis, owners, offsets, counts)
    x_ends = ends(vis)
    weight = pltpu.with_memory_space_constraint(weight, pltpu.VMEM)
    held = pl.pallas_call(
        hold_kernel,
        in_specs=[ANY, VMEM],
        out_specs=VMEM,
        out_shape=tile,
        compiler_params=small,
        cost_estimate=pl.CostEstimate(flops=0, bytes_accessed=2 * weight.size, transcendentals=0),
        name="hold",
    )(weight, held)
    x_inner, held = lax.optimization_barrier((x_inner, held))
    stretches = depth // 3 // 128 * 128
    stretches = (depth - stretches, stretches)
    stretch = depth // 3 // 128 * 128
    sent, later = pl.pallas_call(
        pass_kernel,
        in_specs=[VMEM] * 3,
        out_specs=[VMEM] * 2,
        out_shape=[jax.ShapeDtypeStruct((count, n), BF16) for n in (depth - stretch, stretch)],
        compiler_params=small,
        name="pass",
    )(own, x_inner, vis_gain)
    sent, later, x_outer = lax.optimization_barrier((sent, later, x_outer))
    last_a = far(sent)
    known = (second(info), mirror(info), outer(info), info)
    last_b = far(later)
    cost = pl.CostEstimate(
        flops=2 * 3 * count * depth * columns, bytes_accessed=2 * weight.size, transcendentals=0
    )
    early = pl.pallas_call(
        early_kernel,
        in_specs=[VMEM] * 7,
        out_specs=VMEM,
        out_shape=jax.ShapeDtypeStruct((3 * count, columns), BF16),
        scratch_shapes=[pltpu.VMEM((3 * count, depth), BF16)],
        compiler_params=small,
        cost_estimate=pl.CostEstimate(flops=0, bytes_accessed=0, transcendentals=0),
        name="early",
    )(own, x_outer, x_inner, x_ends, vis_gain, weight, bias)
    pairs = groups // 2
    total = pl.pallas_call(
        late_kernel,
        in_specs=[VMEM] * 3,
        out_specs=VMEM,
        out_shape=jax.ShapeDtypeStruct((count, columns), F32),
        compiler_params=small,
        cost_estimate=pl.CostEstimate(flops=0, bytes_accessed=0, transcendentals=0),
        name="late",
    )(last_a, weight, bias)
    *parts, squares, text_scale = pl.pallas_call(
        functools.partial(project_kernel, groups, cap, size, columns * dp),
        in_specs=[VMEM] * 9,
        out_specs=[VMEM] * (pairs + 2),
        out_shape=[jax.ShapeDtypeStruct((2 * cap * size, columns), BF16)] * pairs
        + [jax.ShapeDtypeStruct((devices, 128), F32), tile],
        scratch_shapes=[
            pltpu.VMEM((dp * count, columns), BF16),
            pltpu.VMEM((count, columns), BF16),
            pltpu.VMEM((dp * count, 128), F32),
        ],
        compiler_params=small,
        cost_estimate=cost,
        name="project",
    )(*known, last_b, weight, total, early, held)
    squares = lax.all_to_all(squares, ("grp", "dp"), 0, 0, tiled=True)
    scales = pl.pallas_call(
        functools.partial(scale_kernel, groups, dp, cap * size, columns * dp),
        in_specs=[VMEM],
        out_specs=VMEM,
        out_shape=jax.ShapeDtypeStruct((128, 128), F32),
        compiler_params=small,
        cost_estimate=pl.CostEstimate(flops=0, bytes_accessed=4 * weight.size, transcendentals=0),
        name="scale",
    )(squares)
    even = [parts[0]] + [across(parts[j], 2 * j) for j in range(1, pairs)]
    *even, scales = lax.optimization_barrier((*even, scales))
    arrived = jax.ShapeDtypeStruct((pairs * cap * size, columns), BF16)
    odd = pl.pallas_call(
        pack_kernel, in_specs=[VMEM] * pairs, out_specs=VMEM, out_shape=arrived, compiler_params=small, name="pack"
    )(*even)
    odd = across(odd, 1)
    gain = out_gain[None, :]
    base, order = pl.pallas_call(
        functools.partial(base_kernel, groups, cap, size),
        in_specs=[VMEM] * (4 + pairs),
        out_specs=[VMEM] * 2,
        out_shape=[
            jax.ShapeDtypeStruct(text.shape, BF16),
            jax.ShapeDtypeStruct((seq_len, pairs * cap * size), BF16),
        ],
        scratch_shapes=[pltpu.VMEM(arrived.shape, BF16)],
        compiler_params=small,
        cost_estimate=pl.CostEstimate(flops=0, bytes_accessed=2 * weight.size, transcendentals=0),
        name="base",
    )(scales, text_scale, gain, text, *even)
    return pl.pallas_call(
        functools.partial(place_kernel, groups, cap, size),
        in_specs=[VMEM] * 5,
        out_specs=ANY,
        out_shape=jax.ShapeDtypeStruct(text.shape, BF16),
        scratch_shapes=[
            pltpu.VMEM(arrived.shape, BF16),
            pltpu.VMEM(text.shape, BF16),
            pltpu.SemaphoreType.DMA((4,)),
        ],
        compiler_params=small,
        name="place",
    )(scales, gain, odd, base, order)


def general(
    vis_features, vis_gain, proj_weight, proj_bias, text_embed, out_gain, image_counts, owner_block, offsets
):
    groups = lax.axis_size("grp")
    width = proj_weight.shape[1] * lax.axis_size("dp")
    slots_device = owner_block.shape[0]
    per_image = vis_features.shape[0] // slots_device
    columns = proj_weight.shape[1]
    seq_len = text_embed.shape[0]
    capacity = seq_len // (groups * per_image)
    features_f = vis_features.astype(jnp.float32)
    normed = (
        features_f
        * lax.rsqrt(jnp.mean(features_f * features_f, axis=-1, keepdims=True) + EPS_VIS)
        * vis_gain
    ).astype(jnp.bfloat16)
    slot_local = jnp.arange(slots_device, dtype=jnp.int32)
    live_offsets = jnp.where(slot_local < image_counts[0], offsets, -1)
    block_owner, block_offsets = (
        lax.all_gather(owner_block, "dp", axis=0, tiled=True),
        lax.all_gather(live_offsets, "dp", axis=0, tiled=True),
    )
    projected = (
        jnp.dot(
            lax.all_gather(normed, "dp", axis=0, tiled=True),
            proj_weight,
            preferred_element_type=jnp.float32,
        )
        + proj_bias
    ).astype(jnp.bfloat16)
    block_slots = block_owner.shape[0]
    earlier = jnp.arange(block_slots)[:, None] > jnp.arange(block_slots)[None, :]
    same_owner = block_owner[:, None] == block_owner[None, :]
    rank_in = jnp.sum(same_owner & earlier, axis=1)
    bucket = block_owner * capacity + rank_in
    selector = jnp.arange(groups * capacity, dtype=jnp.int32)[:, None] == bucket[None, :]
    flat_rows = projected.reshape(block_slots, per_image * columns)
    bucketed = jnp.dot(
        selector.astype(jnp.bfloat16), flat_rows, preferred_element_type=jnp.float32
    ).astype(jnp.bfloat16)
    bucketed = bucketed.reshape(groups, capacity * per_image * columns)
    bucket_offsets = jnp.max(jnp.where(selector, block_offsets[None, :], -1), axis=1).reshape(
        groups, capacity
    )
    arrived, arrived_offsets = (
        lax.all_to_all(bucketed, "grp", split_axis=0, concat_axis=0, tiled=True),
        lax.all_to_all(bucket_offsets, "grp", split_axis=0, concat_axis=0, tiled=True),
    )
    received = arrived.reshape(groups * capacity * per_image, columns)
    starts = arrived_offsets.reshape(groups * capacity)
    target = jnp.where(
        starts[:, None] >= 0,
        starts[:, None] + jnp.arange(per_image, dtype=jnp.int32)[None, :],
        seq_len,
    )
    target = target.reshape(-1).astype(jnp.int32)
    merged = text_embed.at[target].set(received, mode="drop")
    local_squares = jnp.sum(jnp.square(merged.astype(jnp.float32)), axis=1)
    row_total = lax.psum(local_squares, "dp")
    inverse_rms = lax.rsqrt(row_total / width + EPS_OUT)
    hidden = merged.astype(jnp.float32) * inverse_rms[:, None] * out_gain
    return hidden.astype(jnp.bfloat16)


def on_device(vis, vis_gain, weight, bias, text, out_gain, counts, owners, offsets):
    groups, dp = lax.axis_size("grp"), lax.axis_size("dp")
    per_image = vis.shape[0] // owners.shape[0]
    cap = text.shape[0] // (groups * per_image)
    full = dp * owners.shape[0] == groups * cap and groups * cap * per_image == text.shape[0]
    fits = dp == 4 and groups & (groups - 1) == 0 and per_image == 16 and cap == 2 and text.shape[0] <= 512 and 3 * owners.shape[0] <= TEXT
    fits = fits and owners.shape[0] % 4 == 0 and weight.shape[1] % 1024 == 0
    form = fast if full and fits else general
    return form(vis, vis_gain, weight, bias, text, out_gain, counts, owners, offsets)


def solution(mesh):
    return jax.shard_map(
        on_device,
        mesh=mesh,
        in_specs=(
            P(("grp", "dp"), None),
            P(),
            P(None, "dp"),
            P("dp"),
            P("grp", "dp"),
            P("dp"),
            P(("grp", "dp")),
            P(("grp", "dp")),
            P(("grp", "dp")),
        ),
        out_specs=P("grp", "dp"),
        check_vma=False,
    )
```

```python
import functools

import jax
import jax.numpy as jnp
from jax import lax
from jax.experimental import pallas as pl
from jax.experimental.pallas import tpu as pltpu
from jax.sharding import PartitionSpec as P

EPS_VIS = 1e-06
EPS_OUT = 1e-05
TILE = (8, 128)
TEXT = 64
F32 = jnp.float32
BF16 = jnp.bfloat16
VMEM = pl.BlockSpec(memory_space=pltpu.VMEM)
SMEM = pl.BlockSpec(memory_space=pltpu.SMEM)
ANY = pl.BlockSpec(memory_space=pl.ANY)
LIMIT = 16 << 20


def lanes():
    return lax.broadcasted_iota(jnp.int32, TILE, 1)


def tables_kernel(slots, size, text, vis, owners, offsets, counts, info, own, squares):
    lane = lanes()
    tile = jnp.zeros(TILE, F32)
    for c in range(text.shape[0] // 16):
        x = text[c * 16 : (c + 1) * 16, :].astype(F32)
        sums = jnp.sum(x * x, axis=1, keepdims=True)
        tile = jnp.where(lane == 2 * c, sums[:8], tile)
        tile = jnp.where(lane == 2 * c + 1, sums[8:], tile)
    squares[...] = tile
    row = lax.axis_index("dp")
    known = jnp.zeros(TILE, jnp.int32)
    for i in range(slots):
        code = jnp.where(i < counts[0], offsets[i] // size + 1, 0)
        for n, value in enumerate((owners[i], row * slots + i, code)):
            known = jnp.where(lane == n * slots + i, value, known)
    info[...] = known.astype(F32) + pltpu.roll(tile, TEXT, 1)
    own[...] = vis[...]


def spread(slots, size, tiles):
    lane = lax.broadcasted_iota(jnp.int32, (size, 128), 1)
    rows = []
    for tile in tiles:
        for i in range(slots):
            owner, slot, code = [tile[0:1, n * slots + i : n * slots + i + 1] for n in range(3)]
            rows.append(jnp.where(lane == 0, owner, jnp.where(lane == 1, slot, jnp.where(lane == 2, code, 0))))
    return jnp.concatenate(rows, axis=0)


def pass_kernel(own, inner, gain, sent, later):
    row = lax.axis_index("dp")
    depth, stretch = inner.shape[1], sent.shape[1]
    rows = jnp.where(jnp.logical_or(row == 1, row == 2), inner[...], own[...])
    rows = normed(rows, gain[...].reshape(1, depth))
    sent[...] = rows[:, :stretch]
    later[...] = rows[:, stretch:]


def hold_kernel(weight, tile, out):
    del weight
    out[...] = tile[...]


def normed(rows, gain):
    x = rows.astype(F32)
    scale = lax.rsqrt(jnp.mean(x * x, axis=-1, keepdims=True) + EPS_VIS)
    return (x * scale * gain).astype(BF16)


def early_kernel(own, outer, inner, ends, gain, weight, bias, y, x):
    row = lax.axis_index("dp")
    middle = jnp.logical_or(row == 1, row == 2)
    depth, columns = weight.shape
    count = own.shape[0]
    g = gain[...].reshape(1, depth)
    x[0:count] = normed(own[...], g)
    x[count : 2 * count] = normed(outer[...], g)
    x[2 * count : 3 * count] = normed(jnp.where(middle, inner[...], ends[...]), g)
    block = 256
    for n in range(columns // block):
        at = slice(n * block, (n + 1) * block)
        y[:, at] = (jnp.dot(x[...], weight[:, at], preferred_element_type=F32) + bias[:, at]).astype(BF16)


def late_kernel(last, weight, bias, total):
    depth = last.shape[1]
    total[...] = jnp.dot(last[...], weight[:depth, :], preferred_element_type=F32) + bias[...]


def project_kernel(groups, cap, size, width, i3, i2, i1, i0, last, weight, total, early, text, *rest):
    *parts, tiles, text_scale, y, z, codes = rest
    me = lax.axis_index("grp")
    depth, columns = weight.shape
    stretch = last.shape[1]
    down = spread(last.shape[0] // size, size, [i0[...], i1[...], i2[...], i3[...]])
    rows = down.shape[0]
    across = down.T
    owner_down, slot_down = down[:, 0:1], down[:, 1:2]
    owner, slot = across[0:1, :], across[1:2, :]
    earlier = jnp.logical_and(owner_down == owner, slot_down < slot)
    rank = jnp.sum(earlier.astype(F32), axis=0, keepdims=True).astype(jnp.int32) // size
    place = owner.astype(jnp.int32) ^ me
    position = lax.broadcasted_iota(jnp.int32, (1, rows), 1) % size
    seat = (place * cap + rank) * size + position
    first = position == 0
    image = lax.broadcasted_iota(jnp.int32, (1, rows), 1) // size
    at = [
        pl.multiple_of(jnp.sum(jnp.where(jnp.logical_and(first, image == i), seat, 0)), size)
        for i in range(rows // size)
    ]
    block = 256
    for n in range(columns // block):
        part = slice(n * block, (n + 1) * block)
        more = jnp.dot(last[...], weight[depth - stretch :, part], preferred_element_type=F32)
        z[:, part] = (total[:, part] + more).astype(BF16)
    count = early.shape[0] // size
    for i in range(rows // size):
        source, n = (early, i) if i < count else (z, i - count)
        y[pl.ds(at[i], size), :] = source[n * size : (n + 1) * size]
        codes[pl.ds(at[i], size), :] = down[i * size : (i + 1) * size]
    chunk = rows // len(parts)
    for m, part in enumerate(parts):
        part[...] = y[m * chunk : (m + 1) * chunk]
    lane = lanes()
    others = pltpu.roll(i1[...] + i2[...] + i3[...], 128 - TEXT, 1)
    text_scale[...] = lax.rsqrt((text[...] + others) / width + EPS_OUT)
    columns = []
    for k in range(groups):
        wide = y[k * cap * size : (k + 1) * cap * size, :].astype(F32)
        sums = jnp.sum(wide * wide, axis=1, keepdims=True)
        code = [codes[(k * cap + r) * size : (k * cap + r) * size + 1, 2:3] for r in range(cap)]
        fill = jnp.zeros((128 - cap * size - cap, 1), F32)
        columns.append(jnp.concatenate([sums, *code, fill], axis=0))
    lane = lax.broadcasted_iota(jnp.int32, (128, 128), 1)
    told = jnp.zeros((128, 128), F32)
    for k in range(groups):
        told = jnp.where(lane == k, columns[k], told)
    told = told.T
    copies = tiles.shape[0] // groups
    for k in range(groups):
        for q in range(copies):
            tiles[pl.ds((me ^ k) * copies + q, 1), :] = told[k : k + 1, :]


def scale_kernel(groups, dp, rows, width, squares, scales):
    me = lax.axis_index("grp")
    source = lax.broadcasted_iota(jnp.int32, squares.shape, 0)
    lane = lax.broadcasted_iota(jnp.int32, (1, 128), 1)
    told = []
    for k in range(groups):
        mine = source // dp == (me ^ k)
        total = jnp.sum(jnp.where(mine, squares[...], 0), axis=0, keepdims=True)
        code = jnp.sum(jnp.where(source == (me ^ k) * dp, squares[...], 0), axis=0, keepdims=True)
        told.append(jnp.where(lane < rows, lax.rsqrt(total / width + EPS_OUT), code))
    told.append(jnp.zeros((128 - groups, 128), F32))
    scales[...] = jnp.concatenate(told, axis=0).T


def pack_kernel(*refs):
    *parts, out = refs
    rows = parts[0].shape[0] // 2
    for n, part in enumerate(parts):
        out[n * rows : (n + 1) * rows, :] = part[rows:, :]


def scaled(cap, size, k, rows, scales, gain):
    out = []
    for r in range(cap):
        inverse = scales[r * size : (r + 1) * size, k : k + 1]
        out.append((rows[r * size : (r + 1) * size, :].astype(F32) * inverse * gain).astype(BF16))
    return out


def moves(seq_len, cap, size, senders, scales):
    at = cap * size
    codes = [
        jnp.broadcast_to(scales[at + r : at + r + 1, k : k + 1], TILE)
        for k in senders
        for r in range(cap)
        for _ in range(size // 8)
    ]
    code = jnp.concatenate(codes, axis=0).T[0:1, :].astype(jnp.int32)
    position = lax.broadcasted_iota(jnp.int32, code.shape, 1) % size
    target = jnp.where(code > 0, (code - 1) * size + position, -1)
    return (lax.broadcasted_iota(jnp.int32, (seq_len, code.shape[1]), 0) == target).astype(F32)


def base_kernel(groups, cap, size, scales, text_scale, gain, text, *rest):
    *even, out, rows, done, sem = rest
    seq_len = text.shape[0]
    g = gain[...]
    order = moves(seq_len, cap, size, range(0, groups, 2), scales)
    covered = jnp.sum(order, axis=1, keepdims=True)
    for n, part in enumerate(even):
        for r, x in enumerate(scaled(cap, size, 2 * n, part, scales, g)):
            at = (n * cap + r) * size
            rows[at : at + size, :] = x
    moved = jnp.dot(order.astype(BF16), rows[...], preferred_element_type=F32)
    for c in range(seq_len // 16):
        inverse = jnp.concatenate([text_scale[:, 2 * c : 2 * c + 1], text_scale[:, 2 * c + 1 : 2 * c + 2]], axis=0)
        part = slice(c * 16, (c + 1) * 16)
        x = text[part, :].astype(F32) * inverse * g
        done[part, :] = jnp.where(covered[part] > 0, moved[part], x).astype(BF16)
    copy = pltpu.make_async_copy(done, out, sem)
    copy.start()
    copy.wait()


def place_kernel(groups, cap, size, scales, gain, odd, base, out, done, sems):
    del base
    at = cap * size
    g = gain[...]
    places = [(n, k, r) for n, k in enumerate(range(1, groups, 2)) for r in range(cap)]
    starts = [jnp.sum(scales[at + r : at + r + 1, k : k + 1]).astype(jnp.int32) - 1 for _, k, r in places]

    def copy(m):
        there = pl.ds(pl.multiple_of(starts[m] * size, size), size)
        return pltpu.make_async_copy(done.at[m * size : (m + 1) * size], out.at[there], sems.at[m])

    for m, (n, k, r) in enumerate(places):
        if r == 0:
            rows = scaled(cap, size, k, odd[n * at : (n + 1) * at], scales, g)
        done[m * size : (m + 1) * size, :] = rows[r]

        @pl.when(starts[m] >= 0)
        def _():
            copy(m).start()

    for m in range(len(places)):

        @pl.when(starts[m] >= 0)
        def _():
            copy(m).wait()


def outer(x):
    return lax.ppermute(x, "dp", [(0, 1), (1, 0), (2, 3), (3, 2)])


def inner(x):
    return lax.ppermute(x, "dp", [(1, 2), (2, 1), (0, 0), (3, 3)])


def ends(x):
    return lax.ppermute(x, "dp", [(0, 3), (3, 0), (1, 1), (2, 2)])


def mirror(x):
    return lax.ppermute(x, "dp", [(0, 3), (1, 2), (2, 1), (3, 0)])


def second(x):
    return lax.ppermute(x, "dp", [(0, 2), (1, 3), (2, 0), (3, 1)])


def far(x):
    return lax.ppermute(x, "dp", [(0, 2), (1, 0), (2, 3), (3, 1)])


def across(x, k):
    return lax.ppermute(x, "grp", [(i, i ^ k) for i in range(lax.axis_size("grp"))])


def fast(vis, vis_gain, weight, bias, text, out_gain, counts, owners, offsets):
    groups, dp = lax.axis_size("grp"), lax.axis_size("dp")
    devices = groups * dp
    slots = owners.shape[0]
    size = vis.shape[0] // slots
    seq_len, columns = text.shape
    cap = seq_len // (groups * size)
    depth = vis.shape[1]
    small = pltpu.CompilerParams(vmem_limit_bytes=LIMIT)
    count = slots * size
    tile = jax.ShapeDtypeStruct(TILE, F32)
    bias = bias[None, :]

    x_inner, x_outer = inner(vis), outer(vis)
    info, own, held = pl.pallas_call(
        functools.partial(tables_kernel, slots, size),
        in_specs=[VMEM, VMEM, SMEM, SMEM, SMEM],
        out_specs=[VMEM] * 3,
        out_shape=[tile, jax.ShapeDtypeStruct(vis.shape, BF16), tile],
        compiler_params=small,
        name="tables",
    )(text, vis, owners, offsets, counts)
    x_ends = ends(vis)
    weight = pltpu.with_memory_space_constraint(weight, pltpu.VMEM)
    held = pl.pallas_call(
        hold_kernel,
        in_specs=[ANY, VMEM],
        out_specs=VMEM,
        out_shape=tile,
        compiler_params=small,
        cost_estimate=pl.CostEstimate(flops=0, bytes_accessed=2 * weight.size, transcendentals=0),
        name="hold",
    )(weight, held)
    x_inner, held = lax.optimization_barrier((x_inner, held))
    stretches = depth // 3 // 128 * 128
    stretches = (depth - stretches, stretches)
    stretch = depth // 3 // 128 * 128
    sent, later = pl.pallas_call(
        pass_kernel,
        in_specs=[VMEM] * 3,
        out_specs=[VMEM] * 2,
        out_shape=[jax.ShapeDtypeStruct((count, n), BF16) for n in (depth - stretch, stretch)],
        compiler_params=small,
        name="pass",
    )(own, x_inner, vis_gain)
    sent, later, x_outer = lax.optimization_barrier((sent, later, x_outer))
    last_a = far(sent)
    known = (second(info), mirror(info), outer(info), info)
    last_b = far(later)
    cost = pl.CostEstimate(
        flops=2 * 3 * count * depth * columns, bytes_accessed=2 * weight.size, transcendentals=0
    )
    early = pl.pallas_call(
        early_kernel,
        in_specs=[VMEM] * 7,
        out_specs=VMEM,
        out_shape=jax.ShapeDtypeStruct((3 * count, columns), BF16),
        scratch_shapes=[pltpu.VMEM((3 * count, depth), BF16)],
        compiler_params=small,
        cost_estimate=pl.CostEstimate(flops=0, bytes_accessed=0, transcendentals=0),
        name="early",
    )(own, x_outer, x_inner, x_ends, vis_gain, weight, bias)
    pairs = groups // 2
    total = pl.pallas_call(
        late_kernel,
        in_specs=[VMEM] * 3,
        out_specs=VMEM,
        out_shape=jax.ShapeDtypeStruct((count, columns), F32),
        compiler_params=small,
        cost_estimate=pl.CostEstimate(flops=0, bytes_accessed=0, transcendentals=0),
        name="late",
    )(last_a, weight, bias)
    *parts, squares, text_scale = pl.pallas_call(
        functools.partial(project_kernel, groups, cap, size, columns * dp),
        in_specs=[VMEM] * 9,
        out_specs=[VMEM] * (pairs + 2),
        out_shape=[jax.ShapeDtypeStruct((2 * cap * size, columns), BF16)] * pairs
        + [jax.ShapeDtypeStruct((devices, 128), F32), tile],
        scratch_shapes=[
            pltpu.VMEM((dp * count, columns), BF16),
            pltpu.VMEM((count, columns), BF16),
            pltpu.VMEM((dp * count, 128), F32),
        ],
        compiler_params=small,
        cost_estimate=cost,
        name="project",
    )(*known, last_b, weight, total, early, held)
    squares = lax.all_to_all(squares, ("grp", "dp"), 0, 0, tiled=True)
    scales = pl.pallas_call(
        functools.partial(scale_kernel, groups, dp, cap * size, columns * dp),
        in_specs=[VMEM],
        out_specs=VMEM,
        out_shape=jax.ShapeDtypeStruct((128, 128), F32),
        compiler_params=small,
        cost_estimate=pl.CostEstimate(flops=0, bytes_accessed=4 * weight.size, transcendentals=0),
        name="scale",
    )(squares)
    even = [parts[0]] + [across(parts[j], 2 * j) for j in range(1, pairs)]
    *even, squares = lax.optimization_barrier((*even, squares))
    arrived = jax.ShapeDtypeStruct((pairs * cap * size, columns), BF16)
    odd = pl.pallas_call(
        pack_kernel, in_specs=[VMEM] * pairs, out_specs=VMEM, out_shape=arrived, compiler_params=small, name="pack"
    )(*even)
    odd = across(odd, 1)
    gain = out_gain[None, :]
    base = pl.pallas_call(
        functools.partial(base_kernel, groups, cap, size),
        in_specs=[VMEM] * (4 + pairs),
        out_specs=ANY,
        out_shape=jax.ShapeDtypeStruct(text.shape, BF16),
        scratch_shapes=[pltpu.VMEM(arrived.shape, BF16), pltpu.VMEM(text.shape, BF16), pltpu.SemaphoreType.DMA],
        compiler_params=small,
        cost_estimate=pl.CostEstimate(flops=0, bytes_accessed=2 * weight.size, transcendentals=0),
        name="base",
    )(scales, text_scale, gain, text, *even)
    return pl.pallas_call(
        functools.partial(place_kernel, groups, cap, size),
        in_specs=[VMEM] * 3 + [ANY],
        out_specs=ANY,
        out_shape=jax.ShapeDtypeStruct(text.shape, BF16),
        input_output_aliases={3: 0},
        scratch_shapes=[pltpu.VMEM(arrived.shape, BF16), pltpu.SemaphoreType.DMA((pairs * cap,))],
        compiler_params=small,
        name="place",
    )(scales, gain, odd, base)


def general(
    vis_features, vis_gain, proj_weight, proj_bias, text_embed, out_gain, image_counts, owner_block, offsets
):
    groups = lax.axis_size("grp")
    width = proj_weight.shape[1] * lax.axis_size("dp")
    slots_device = owner_block.shape[0]
    per_image = vis_features.shape[0] // slots_device
    columns = proj_weight.shape[1]
    seq_len = text_embed.shape[0]
    capacity = seq_len // (groups * per_image)
    features_f = vis_features.astype(jnp.float32)
    normed = (
        features_f
        * lax.rsqrt(jnp.mean(features_f * features_f, axis=-1, keepdims=True) + EPS_VIS)
        * vis_gain
    ).astype(jnp.bfloat16)
    slot_local = jnp.arange(slots_device, dtype=jnp.int32)
    live_offsets = jnp.where(slot_local < image_counts[0], offsets, -1)
    block_owner, block_offsets = (
        lax.all_gather(owner_block, "dp", axis=0, tiled=True),
        lax.all_gather(live_offsets, "dp", axis=0, tiled=True),
    )
    projected = (
        jnp.dot(
            lax.all_gather(normed, "dp", axis=0, tiled=True),
            proj_weight,
            preferred_element_type=jnp.float32,
        )
        + proj_bias
    ).astype(jnp.bfloat16)
    block_slots = block_owner.shape[0]
    earlier = jnp.arange(block_slots)[:, None] > jnp.arange(block_slots)[None, :]
    same_owner = block_owner[:, None] == block_owner[None, :]
    rank_in = jnp.sum(same_owner & earlier, axis=1)
    bucket = block_owner * capacity + rank_in
    selector = jnp.arange(groups * capacity, dtype=jnp.int32)[:, None] == bucket[None, :]
    flat_rows = projected.reshape(block_slots, per_image * columns)
    bucketed = jnp.dot(
        selector.astype(jnp.bfloat16), flat_rows, preferred_element_type=jnp.float32
    ).astype(jnp.bfloat16)
    bucketed = bucketed.reshape(groups, capacity * per_image * columns)
    bucket_offsets = jnp.max(jnp.where(selector, block_offsets[None, :], -1), axis=1).reshape(
        groups, capacity
    )
    arrived, arrived_offsets = (
        lax.all_to_all(bucketed, "grp", split_axis=0, concat_axis=0, tiled=True),
        lax.all_to_all(bucket_offsets, "grp", split_axis=0, concat_axis=0, tiled=True),
    )
    received = arrived.reshape(groups * capacity * per_image, columns)
    starts = arrived_offsets.reshape(groups * capacity)
    target = jnp.where(
        starts[:, None] >= 0,
        starts[:, None] + jnp.arange(per_image, dtype=jnp.int32)[None, :],
        seq_len,
    )
    target = target.reshape(-1).astype(jnp.int32)
    merged = text_embed.at[target].set(received, mode="drop")
    local_squares = jnp.sum(jnp.square(merged.astype(jnp.float32)), axis=1)
    row_total = lax.psum(local_squares, "dp")
    inverse_rms = lax.rsqrt(row_total / width + EPS_OUT)
    hidden = merged.astype(jnp.float32) * inverse_rms[:, None] * out_gain
    return hidden.astype(jnp.bfloat16)


def on_device(vis, vis_gain, weight, bias, text, out_gain, counts, owners, offsets):
    groups, dp = lax.axis_size("grp"), lax.axis_size("dp")
    per_image = vis.shape[0] // owners.shape[0]
    cap = text.shape[0] // (groups * per_image)
    full = dp * owners.shape[0] == groups * cap and groups * cap * per_image == text.shape[0]
    fits = dp == 4 and groups & (groups - 1) == 0 and per_image == 16 and cap == 2 and text.shape[0] <= 512 and 3 * owners.shape[0] <= TEXT
    fits = fits and owners.shape[0] % 4 == 0 and weight.shape[1] % 1024 == 0
    form = fast if full and fits else general
    return form(vis, vis_gain, weight, bias, text, out_gain, counts, owners, offsets)


def solution(mesh):
    return jax.shard_map(
        on_device,
        mesh=mesh,
        in_specs=(
            P(("grp", "dp"), None),
            P(),
            P(None, "dp"),
            P("dp"),
            P("grp", "dp"),
            P("dp"),
            P(("grp", "dp")),
            P(("grp", "dp")),
            P(("grp", "dp")),
        ),
        out_specs=P("grp", "dp"),
        check_vma=False,
    )
```

```python
import functools

import jax
import jax.numpy as jnp
from jax import lax
from jax.experimental import pallas as pl
from jax.experimental.pallas import tpu as pltpu
from jax.sharding import PartitionSpec as P

EPS_VIS = 1e-06
EPS_OUT = 1e-05
TILE = (8, 128)
TEXT = 64
F32 = jnp.float32
BF16 = jnp.bfloat16
VMEM = pl.BlockSpec(memory_space=pltpu.VMEM)
SMEM = pl.BlockSpec(memory_space=pltpu.SMEM)
ANY = pl.BlockSpec(memory_space=pl.ANY)
LIMIT = 16 << 20


def lanes():
    return lax.broadcasted_iota(jnp.int32, TILE, 1)


def tables_kernel(slots, size, text, vis, owners, offsets, counts, info, own, squares):
    lane = lanes()
    tile = jnp.zeros(TILE, F32)
    for c in range(text.shape[0] // 16):
        x = text[c * 16 : (c + 1) * 16, :].astype(F32)
        sums = jnp.sum(x * x, axis=1, keepdims=True)
        tile = jnp.where(lane == 2 * c, sums[:8], tile)
        tile = jnp.where(lane == 2 * c + 1, sums[8:], tile)
    squares[...] = tile
    row = lax.axis_index("dp")
    known = jnp.zeros(TILE, jnp.int32)
    for i in range(slots):
        code = jnp.where(i < counts[0], offsets[i] // size + 1, 0)
        for n, value in enumerate((owners[i], row * slots + i, code)):
            known = jnp.where(lane == n * slots + i, value, known)
    info[...] = known.astype(F32) + pltpu.roll(tile, TEXT, 1)
    own[...] = vis[...]


def spread(slots, size, tiles):
    lane = lax.broadcasted_iota(jnp.int32, (size, 128), 1)
    rows = []
    for tile in tiles:
        for i in range(slots):
            owner, slot, code = [tile[0:1, n * slots + i : n * slots + i + 1] for n in range(3)]
            rows.append(jnp.where(lane == 0, owner, jnp.where(lane == 1, slot, jnp.where(lane == 2, code, 0))))
    return jnp.concatenate(rows, axis=0)


def pass_kernel(own, inner, gain, sent, later):
    row = lax.axis_index("dp")
    depth, stretch = inner.shape[1], sent.shape[1]
    rows = jnp.where(jnp.logical_or(row == 1, row == 2), inner[...], own[...])
    rows = normed(rows, gain[...].reshape(1, depth))
    sent[...] = rows[:, :stretch]
    later[...] = rows[:, stretch:]


def hold_kernel(weight, tile, out):
    del weight
    out[...] = tile[...]


def normed(rows, gain):
    x = rows.astype(F32)
    scale = lax.rsqrt(jnp.mean(x * x, axis=-1, keepdims=True) + EPS_VIS)
    return (x * scale * gain).astype(BF16)


def early_kernel(own, outer, inner, ends, gain, weight, bias, y, x):
    row = lax.axis_index("dp")
    middle = jnp.logical_or(row == 1, row == 2)
    depth, columns = weight.shape
    count = own.shape[0]
    g = gain[...].reshape(1, depth)
    x[0:count] = normed(own[...], g)
    x[count : 2 * count] = normed(outer[...], g)
    x[2 * count : 3 * count] = normed(jnp.where(middle, inner[...], ends[...]), g)
    block = 256
    for n in range(columns // block):
        at = slice(n * block, (n + 1) * block)
        y[:, at] = (jnp.dot(x[...], weight[:, at], preferred_element_type=F32) + bias[:, at]).astype(BF16)


def late_kernel(last, weight, bias, total):
    depth = last.shape[1]
    total[...] = jnp.dot(last[...], weight[:depth, :], preferred_element_type=F32) + bias[...]


def project_kernel(groups, cap, size, width, i3, i2, i1, i0, last, weight, total, early, text, *rest):
    *parts, tiles, text_scale, y, z, codes = rest
    me = lax.axis_index("grp")
    depth, columns = weight.shape
    stretch = last.shape[1]
    down = spread(last.shape[0] // size, size, [i0[...], i1[...], i2[...], i3[...]])
    rows = down.shape[0]
    across = down.T
    owner_down, slot_down = down[:, 0:1], down[:, 1:2]
    owner, slot = across[0:1, :], across[1:2, :]
    earlier = jnp.logical_and(owner_down == owner, slot_down < slot)
    rank = jnp.sum(earlier.astype(F32), axis=0, keepdims=True).astype(jnp.int32) // size
    place = owner.astype(jnp.int32) ^ me
    position = lax.broadcasted_iota(jnp.int32, (1, rows), 1) % size
    seat = (place * cap + rank) * size + position
    first = position == 0
    image = lax.broadcasted_iota(jnp.int32, (1, rows), 1) // size
    at = [
        pl.multiple_of(jnp.sum(jnp.where(jnp.logical_and(first, image == i), seat, 0)), size)
        for i in range(rows // size)
    ]
    block = 256
    for n in range(columns // block):
        part = slice(n * block, (n + 1) * block)
        more = jnp.dot(last[...], weight[depth - stretch :, part], preferred_element_type=F32)
        z[:, part] = (total[:, part] + more).astype(BF16)
    count = early.shape[0] // size
    for i in range(rows // size):
        source, n = (early, i) if i < count else (z, i - count)
        y[pl.ds(at[i], size), :] = source[n * size : (n + 1) * size]
        codes[pl.ds(at[i], size), :] = down[i * size : (i + 1) * size]
    chunk = rows // len(parts)
    for m, part in enumerate(parts):
        part[...] = y[m * chunk : (m + 1) * chunk]
    lane = lanes()
    others = pltpu.roll(i1[...] + i2[...] + i3[...], 128 - TEXT, 1)
    text_scale[...] = lax.rsqrt((text[...] + others) / width + EPS_OUT)
    columns = []
    for k in range(groups):
        wide = y[k * cap * size : (k + 1) * cap * size, :].astype(F32)
        sums = jnp.sum(wide * wide, axis=1, keepdims=True)
        code = [codes[(k * cap + r) * size : (k * cap + r) * size + 1, 2:3] for r in range(cap)]
        fill = jnp.zeros((128 - cap * size - cap, 1), F32)
        columns.append(jnp.concatenate([sums, *code, fill], axis=0))
    lane = lax.broadcasted_iota(jnp.int32, (128, 128), 1)
    told = jnp.zeros((128, 128), F32)
    for k in range(groups):
        told = jnp.where(lane == k, columns[k], told)
    told = told.T
    copies = tiles.shape[0] // groups
    for k in range(groups):
        for q in range(copies):
            tiles[pl.ds((me ^ k) * copies + q, 1), :] = told[k : k + 1, :]


def scale_kernel(groups, dp, rows, width, squares, scales):
    me = lax.axis_index("grp")
    source = lax.broadcasted_iota(jnp.int32, squares.shape, 0)
    lane = lax.broadcasted_iota(jnp.int32, (1, 128), 1)
    told = []
    for k in range(groups):
        mine = source // dp == (me ^ k)
        total = jnp.sum(jnp.where(mine, squares[...], 0), axis=0, keepdims=True)
        code = jnp.sum(jnp.where(source == (me ^ k) * dp, squares[...], 0), axis=0, keepdims=True)
        told.append(jnp.where(lane < rows, lax.rsqrt(total / width + EPS_OUT), code))
    told.append(jnp.zeros((128 - groups, 128), F32))
    scales[...] = jnp.concatenate(told, axis=0).T


def pack_kernel(*refs):
    *parts, out = refs
    rows = parts[0].shape[0] // 2
    for n, part in enumerate(parts):
        out[n * rows : (n + 1) * rows, :] = part[rows:, :]


def scaled(cap, size, k, rows, scales, gain):
    out = []
    for r in range(cap):
        inverse = scales[r * size : (r + 1) * size, k : k + 1]
        out.append((rows[r * size : (r + 1) * size, :].astype(F32) * inverse * gain).astype(BF16))
    return out


def moves(seq_len, cap, size, senders, scales):
    at = cap * size
    codes = [
        jnp.broadcast_to(scales[at + r : at + r + 1, k : k + 1], TILE)
        for k in senders
        for r in range(cap)
        for _ in range(size // 8)
    ]
    code = jnp.concatenate(codes, axis=0).T[0:1, :].astype(jnp.int32)
    position = lax.broadcasted_iota(jnp.int32, code.shape, 1) % size
    target = jnp.where(code > 0, (code - 1) * size + position, -1)
    return (lax.broadcasted_iota(jnp.int32, (seq_len, code.shape[1]), 0) == target).astype(F32)


def base_kernel(groups, cap, size, scales, text_scale, gain, text, *rest):
    *even, out, rows, done, sems = rest
    seq_len = text.shape[0]
    g = gain[...]
    order = moves(seq_len, cap, size, range(0, groups, 2), scales)
    covered = jnp.sum(order, axis=1, keepdims=True)
    for n, part in enumerate(even):
        for r, x in enumerate(scaled(cap, size, 2 * n, part, scales, g)):
            at = (n * cap + r) * size
            rows[at : at + size, :] = x
    moved = jnp.dot(order.astype(BF16), rows[...], preferred_element_type=F32)
    copies, stretch = [], seq_len // sems.shape[0]
    for c in range(seq_len // 16):
        inverse = jnp.concatenate([text_scale[:, 2 * c : 2 * c + 1], text_scale[:, 2 * c + 1 : 2 * c + 2]], axis=0)
        part = slice(c * 16, (c + 1) * 16)
        x = text[part, :].astype(F32) * inverse * g
        done[part, :] = jnp.where(covered[part] > 0, moved[part], x).astype(BF16)
        if (c + 1) * 16 % stretch == 0:
            there = slice((c + 1) * 16 - stretch, (c + 1) * 16)
            copies.append(pltpu.make_async_copy(done.at[there], out.at[there], sems.at[len(copies)]))
            copies[-1].start()
    for copy in copies:
        copy.wait()


def place_kernel(groups, cap, size, scales, gain, odd, base, out, done, sems):
    del base
    at = cap * size
    g = gain[...]
    places = [(n, k, r) for n, k in enumerate(range(1, groups, 2)) for r in range(cap)]
    starts = [jnp.sum(scales[at + r : at + r + 1, k : k + 1]).astype(jnp.int32) - 1 for _, k, r in places]

    def copy(m):
        there = pl.ds(pl.multiple_of(starts[m] * size, size), size)
        return pltpu.make_async_copy(done.at[m * size : (m + 1) * size], out.at[there], sems.at[m])

    for m, (n, k, r) in enumerate(places):
        if r == 0:
            rows = scaled(cap, size, k, odd[n * at : (n + 1) * at], scales, g)
        done[m * size : (m + 1) * size, :] = rows[r]

        @pl.when(starts[m] >= 0)
        def _():
            copy(m).start()

    for m in range(len(places)):

        @pl.when(starts[m] >= 0)
        def _():
            copy(m).wait()


def outer(x):
    return lax.ppermute(x, "dp", [(0, 1), (1, 0), (2, 3), (3, 2)])


def inner(x):
    return lax.ppermute(x, "dp", [(1, 2), (2, 1), (0, 0), (3, 3)])


def ends(x):
    return lax.ppermute(x, "dp", [(0, 3), (3, 0), (1, 1), (2, 2)])


def mirror(x):
    return lax.ppermute(x, "dp", [(0, 3), (1, 2), (2, 1), (3, 0)])


def second(x):
    return lax.ppermute(x, "dp", [(0, 2), (1, 3), (2, 0), (3, 1)])


def far(x):
    return lax.ppermute(x, "dp", [(0, 2), (1, 0), (2, 3), (3, 1)])


def across(x, k):
    return lax.ppermute(x, "grp", [(i, i ^ k) for i in range(lax.axis_size("grp"))])


def fast(vis, vis_gain, weight, bias, text, out_gain, counts, owners, offsets):
    groups, dp = lax.axis_size("grp"), lax.axis_size("dp")
    devices = groups * dp
    slots = owners.shape[0]
    size = vis.shape[0] // slots
    seq_len, columns = text.shape
    cap = seq_len // (groups * size)
    depth = vis.shape[1]
    small = pltpu.CompilerParams(vmem_limit_bytes=LIMIT)
    count = slots * size
    tile = jax.ShapeDtypeStruct(TILE, F32)
    bias = bias[None, :]

    x_inner, x_outer = inner(vis), outer(vis)
    info, own, held = pl.pallas_call(
        functools.partial(tables_kernel, slots, size),
        in_specs=[VMEM, VMEM, SMEM, SMEM, SMEM],
        out_specs=[VMEM] * 3,
        out_shape=[tile, jax.ShapeDtypeStruct(vis.shape, BF16), tile],
        compiler_params=small,
        name="tables",
    )(text, vis, owners, offsets, counts)
    x_ends = ends(vis)
    weight = pltpu.with_memory_space_constraint(weight, pltpu.VMEM)
    held = pl.pallas_call(
        hold_kernel,
        in_specs=[ANY, VMEM],
        out_specs=VMEM,
        out_shape=tile,
        compiler_params=small,
        cost_estimate=pl.CostEstimate(flops=0, bytes_accessed=2 * weight.size, transcendentals=0),
        name="hold",
    )(weight, held)
    x_inner, held = lax.optimization_barrier((x_inner, held))
    stretches = depth // 3 // 128 * 128
    stretches = (depth - stretches, stretches)
    stretch = depth // 4 // 128 * 128
    sent, later = pl.pallas_call(
        pass_kernel,
        in_specs=[VMEM] * 3,
        out_specs=[VMEM] * 2,
        out_shape=[jax.ShapeDtypeStruct((count, n), BF16) for n in (depth - stretch, stretch)],
        compiler_params=small,
        name="pass",
    )(own, x_inner, vis_gain)
    sent, later, x_outer = lax.optimization_barrier((sent, later, x_outer))
    last_a = far(sent)
    known = (second(info), mirror(info), outer(info), info)
    last_b = far(later)
    cost = pl.CostEstimate(
        flops=2 * 3 * count * depth * columns, bytes_accessed=2 * weight.size, transcendentals=0
    )
    early = pl.pallas_call(
        early_kernel,
        in_specs=[VMEM] * 7,
        out_specs=VMEM,
        out_shape=jax.ShapeDtypeStruct((3 * count, columns), BF16),
        scratch_shapes=[pltpu.VMEM((3 * count, depth), BF16)],
        compiler_params=small,
        cost_estimate=pl.CostEstimate(flops=0, bytes_accessed=0, transcendentals=0),
        name="early",
    )(own, x_outer, x_inner, x_ends, vis_gain, weight, bias)
    pairs = groups // 2
    total = pl.pallas_call(
        late_kernel,
        in_specs=[VMEM] * 3,
        out_specs=VMEM,
        out_shape=jax.ShapeDtypeStruct((count, columns), F32),
        compiler_params=small,
        cost_estimate=pl.CostEstimate(flops=0, bytes_accessed=0, transcendentals=0),
        name="late",
    )(last_a, weight, bias)
    *parts, squares, text_scale = pl.pallas_call(
        functools.partial(project_kernel, groups, cap, size, columns * dp),
        in_specs=[VMEM] * 9,
        out_specs=[VMEM] * (pairs + 2),
        out_shape=[jax.ShapeDtypeStruct((2 * cap * size, columns), BF16)] * pairs
        + [jax.ShapeDtypeStruct((devices, 128), F32), tile],
        scratch_shapes=[
            pltpu.VMEM((dp * count, columns), BF16),
            pltpu.VMEM((count, columns), BF16),
            pltpu.VMEM((dp * count, 128), F32),
        ],
        compiler_params=small,
        cost_estimate=cost,
        name="project",
    )(*known, last_b, weight, total, early, held)
    squares = lax.all_to_all(squares, ("grp", "dp"), 0, 0, tiled=True)
    scales = pl.pallas_call(
        functools.partial(scale_kernel, groups, dp, cap * size, columns * dp),
        in_specs=[VMEM],
        out_specs=VMEM,
        out_shape=jax.ShapeDtypeStruct((128, 128), F32),
        compiler_params=small,
        cost_estimate=pl.CostEstimate(flops=0, bytes_accessed=4 * weight.size, transcendentals=0),
        name="scale",
    )(squares)
    even = [parts[0]] + [across(parts[j], 2 * j) for j in range(pairs - 1, 0, -1)][::-1]
    *even, squares = lax.optimization_barrier((*even, squares))
    arrived = jax.ShapeDtypeStruct((pairs * cap * size, columns), BF16)
    odd = pl.pallas_call(
        pack_kernel, in_specs=[VMEM] * pairs, out_specs=VMEM, out_shape=arrived, compiler_params=small, name="pack"
    )(*even)
    odd = across(odd, 1)
    gain = out_gain[None, :]
    base = pl.pallas_call(
        functools.partial(base_kernel, groups, cap, size),
        in_specs=[VMEM] * (4 + pairs),
        out_specs=ANY,
        out_shape=jax.ShapeDtypeStruct(text.shape, BF16),
        scratch_shapes=[pltpu.VMEM(arrived.shape, BF16), pltpu.VMEM(text.shape, BF16), pltpu.SemaphoreType.DMA((4,))],
        compiler_params=small,
        cost_estimate=pl.CostEstimate(flops=0, bytes_accessed=2 * weight.size, transcendentals=0),
        name="base",
    )(scales, text_scale, gain, text, *even)
    return pl.pallas_call(
        functools.partial(place_kernel, groups, cap, size),
        in_specs=[VMEM] * 3 + [ANY],
        out_specs=ANY,
        out_shape=jax.ShapeDtypeStruct(text.shape, BF16),
        input_output_aliases={3: 0},
        scratch_shapes=[pltpu.VMEM(arrived.shape, BF16), pltpu.SemaphoreType.DMA((pairs * cap,))],
        compiler_params=small,
        name="place",
    )(scales, gain, odd, base)


def general(
    vis_features, vis_gain, proj_weight, proj_bias, text_embed, out_gain, image_counts, owner_block, offsets
):
    groups = lax.axis_size("grp")
    width = proj_weight.shape[1] * lax.axis_size("dp")
    slots_device = owner_block.shape[0]
    per_image = vis_features.shape[0] // slots_device
    columns = proj_weight.shape[1]
    seq_len = text_embed.shape[0]
    capacity = seq_len // (groups * per_image)
    features_f = vis_features.astype(jnp.float32)
    normed = (
        features_f
        * lax.rsqrt(jnp.mean(features_f * features_f, axis=-1, keepdims=True) + EPS_VIS)
        * vis_gain
    ).astype(jnp.bfloat16)
    slot_local = jnp.arange(slots_device, dtype=jnp.int32)
    live_offsets = jnp.where(slot_local < image_counts[0], offsets, -1)
    block_owner, block_offsets = (
        lax.all_gather(owner_block, "dp", axis=0, tiled=True),
        lax.all_gather(live_offsets, "dp", axis=0, tiled=True),
    )
    projected = (
        jnp.dot(
            lax.all_gather(normed, "dp", axis=0, tiled=True),
            proj_weight,
            preferred_element_type=jnp.float32,
        )
        + proj_bias
    ).astype(jnp.bfloat16)
    block_slots = block_owner.shape[0]
    earlier = jnp.arange(block_slots)[:, None] > jnp.arange(block_slots)[None, :]
    same_owner = block_owner[:, None] == block_owner[None, :]
    rank_in = jnp.sum(same_owner & earlier, axis=1)
    bucket = block_owner * capacity + rank_in
    selector = jnp.arange(groups * capacity, dtype=jnp.int32)[:, None] == bucket[None, :]
    flat_rows = projected.reshape(block_slots, per_image * columns)
    bucketed = jnp.dot(
        selector.astype(jnp.bfloat16), flat_rows, preferred_element_type=jnp.float32
    ).astype(jnp.bfloat16)
    bucketed = bucketed.reshape(groups, capacity * per_image * columns)
    bucket_offsets = jnp.max(jnp.where(selector, block_offsets[None, :], -1), axis=1).reshape(
        groups, capacity
    )
    arrived, arrived_offsets = (
        lax.all_to_all(bucketed, "grp", split_axis=0, concat_axis=0, tiled=True),
        lax.all_to_all(bucket_offsets, "grp", split_axis=0, concat_axis=0, tiled=True),
    )
    received = arrived.reshape(groups * capacity * per_image, columns)
    starts = arrived_offsets.reshape(groups * capacity)
    target = jnp.where(
        starts[:, None] >= 0,
        starts[:, None] + jnp.arange(per_image, dtype=jnp.int32)[None, :],
        seq_len,
    )
    target = target.reshape(-1).astype(jnp.int32)
    merged = text_embed.at[target].set(received, mode="drop")
    local_squares = jnp.sum(jnp.square(merged.astype(jnp.float32)), axis=1)
    row_total = lax.psum(local_squares, "dp")
    inverse_rms = lax.rsqrt(row_total / width + EPS_OUT)
    hidden = merged.astype(jnp.float32) * inverse_rms[:, None] * out_gain
    return hidden.astype(jnp.bfloat16)


def on_device(vis, vis_gain, weight, bias, text, out_gain, counts, owners, offsets):
    groups, dp = lax.axis_size("grp"), lax.axis_size("dp")
    per_image = vis.shape[0] // owners.shape[0]
    cap = text.shape[0] // (groups * per_image)
    full = dp * owners.shape[0] == groups * cap and groups * cap * per_image == text.shape[0]
    fits = dp == 4 and groups & (groups - 1) == 0 and per_image == 16 and cap == 2 and text.shape[0] <= 512 and 3 * owners.shape[0] <= TEXT
    fits = fits and owners.shape[0] % 4 == 0 and weight.shape[1] % 1024 == 0
    form = fast if full and fits else general
    return form(vis, vis_gain, weight, bias, text, out_gain, counts, owners, offsets)


def solution(mesh):
    return jax.shard_map(
        on_device,
        mesh=mesh,
        in_specs=(
            P(("grp", "dp"), None),
            P(),
            P(None, "dp"),
            P("dp"),
            P("grp", "dp"),
            P("dp"),
            P(("grp", "dp")),
            P(("grp", "dp")),
            P(("grp", "dp")),
        ),
        out_specs=P("grp", "dp"),
        check_vma=False,
    )
```

```python
import functools

import jax
import jax.numpy as jnp
from jax import lax
from jax.experimental import pallas as pl
from jax.experimental.pallas import tpu as pltpu
from jax.sharding import PartitionSpec as P

EPS_VIS = 1e-06
EPS_OUT = 1e-05
TILE = (8, 128)
TEXT = 64
F32 = jnp.float32
BF16 = jnp.bfloat16
VMEM = pl.BlockSpec(memory_space=pltpu.VMEM)
SMEM = pl.BlockSpec(memory_space=pltpu.SMEM)
ANY = pl.BlockSpec(memory_space=pl.ANY)
LIMIT = 16 << 20


def lanes():
    return lax.broadcasted_iota(jnp.int32, TILE, 1)


def tables_kernel(slots, size, text, vis, owners, offsets, counts, info, own, squares):
    lane = lanes()
    tile = jnp.zeros(TILE, F32)
    for c in range(text.shape[0] // 16):
        x = text[c * 16 : (c + 1) * 16, :].astype(F32)
        sums = jnp.sum(x * x, axis=1, keepdims=True)
        tile = jnp.where(lane == 2 * c, sums[:8], tile)
        tile = jnp.where(lane == 2 * c + 1, sums[8:], tile)
    squares[...] = tile
    row = lax.axis_index("dp")
    known = jnp.zeros(TILE, jnp.int32)
    for i in range(slots):
        code = jnp.where(i < counts[0], offsets[i] // size + 1, 0)
        for n, value in enumerate((owners[i], row * slots + i, code)):
            known = jnp.where(lane == n * slots + i, value, known)
    info[...] = known.astype(F32) + pltpu.roll(tile, TEXT, 1)
    own[...] = vis[...]


def spread(slots, size, tiles):
    lane = lax.broadcasted_iota(jnp.int32, (size, 128), 1)
    rows = []
    for tile in tiles:
        for i in range(slots):
            owner, slot, code = [tile[0:1, n * slots + i : n * slots + i + 1] for n in range(3)]
            rows.append(jnp.where(lane == 0, owner, jnp.where(lane == 1, slot, jnp.where(lane == 2, code, 0))))
    return jnp.concatenate(rows, axis=0)


def pass_kernel(own, inner, gain, sent, later):
    row = lax.axis_index("dp")
    depth, stretch = inner.shape[1], sent.shape[1]
    rows = jnp.where(jnp.logical_or(row == 1, row == 2), inner[...], own[...])
    rows = normed(rows, gain[...].reshape(1, depth))
    sent[...] = rows[:, :stretch]
    later[...] = rows[:, stretch:]


def hold_kernel(weight, tile, out):
    del weight
    out[...] = tile[...]


def normed(rows, gain):
    x = rows.astype(F32)
    scale = lax.rsqrt(jnp.mean(x * x, axis=-1, keepdims=True) + EPS_VIS)
    return (x * scale * gain).astype(BF16)


def early_kernel(own, outer, inner, ends, gain, weight, bias, y, x):
    row = lax.axis_index("dp")
    middle = jnp.logical_or(row == 1, row == 2)
    depth, columns = weight.shape
    count = own.shape[0]
    g = gain[...].reshape(1, depth)
    x[0:count] = normed(own[...], g)
    x[count : 2 * count] = normed(outer[...], g)
    x[2 * count : 3 * count] = normed(jnp.where(middle, inner[...], ends[...]), g)
    block = 256
    for n in range(columns // block):
        at = slice(n * block, (n + 1) * block)
        y[:, at] = (jnp.dot(x[...], weight[:, at], preferred_element_type=F32) + bias[:, at]).astype(BF16)


def late_kernel(last, weight, bias, total):
    depth = last.shape[1]
    total[...] = jnp.dot(last[...], weight[:depth, :], preferred_element_type=F32) + bias[...]


def project_kernel(groups, cap, size, width, i3, i2, i1, i0, last, weight, total, early, text, *rest):
    *parts, tiles, text_scale, y, z, codes = rest
    me = lax.axis_index("grp")
    depth, columns = weight.shape
    stretch = last.shape[1]
    down = spread(last.shape[0] // size, size, [i0[...], i1[...], i2[...], i3[...]])
    rows = down.shape[0]
    across = down.T
    owner_down, slot_down = down[:, 0:1], down[:, 1:2]
    owner, slot = across[0:1, :], across[1:2, :]
    earlier = jnp.logical_and(owner_down == owner, slot_down < slot)
    rank = jnp.sum(earlier.astype(F32), axis=0, keepdims=True).astype(jnp.int32) // size
    place = owner.astype(jnp.int32) ^ me
    position = lax.broadcasted_iota(jnp.int32, (1, rows), 1) % size
    seat = (place * cap + rank) * size + position
    first = position == 0
    image = lax.broadcasted_iota(jnp.int32, (1, rows), 1) // size
    at = [
        pl.multiple_of(jnp.sum(jnp.where(jnp.logical_and(first, image == i), seat, 0)), size)
        for i in range(rows // size)
    ]
    block = 256
    for n in range(columns // block):
        part = slice(n * block, (n + 1) * block)
        more = jnp.dot(last[...], weight[depth - stretch :, part], preferred_element_type=F32)
        z[:, part] = (total[:, part] + more).astype(BF16)
    count = early.shape[0] // size
    for i in range(rows // size):
        source, n = (early, i) if i < count else (z, i - count)
        y[pl.ds(at[i], size), :] = source[n * size : (n + 1) * size]
        codes[pl.ds(at[i], size), :] = down[i * size : (i + 1) * size]
    chunk = rows // len(parts)
    for m, part in enumerate(parts):
        part[...] = y[m * chunk : (m + 1) * chunk]
    lane = lanes()
    others = pltpu.roll(i1[...] + i2[...] + i3[...], 128 - TEXT, 1)
    text_scale[...] = lax.rsqrt((text[...] + others) / width + EPS_OUT)
    columns = []
    for k in range(groups):
        wide = y[k * cap * size : (k + 1) * cap * size, :].astype(F32)
        sums = jnp.sum(wide * wide, axis=1, keepdims=True)
        code = [codes[(k * cap + r) * size : (k * cap + r) * size + 1, 2:3] for r in range(cap)]
        fill = jnp.zeros((128 - cap * size - cap, 1), F32)
        columns.append(jnp.concatenate([sums, *code, fill], axis=0))
    lane = lax.broadcasted_iota(jnp.int32, (128, 128), 1)
    told = jnp.zeros((128, 128), F32)
    for k in range(groups):
        told = jnp.where(lane == k, columns[k], told)
    told = told.T
    copies = tiles.shape[0] // groups
    for k in range(groups):
        for q in range(copies):
            tiles[pl.ds((me ^ k) * copies + q, 1), :] = told[k : k + 1, :]


def scale_kernel(groups, dp, rows, width, squares, scales):
    me = lax.axis_index("grp")
    source = lax.broadcasted_iota(jnp.int32, squares.shape, 0)
    lane = lax.broadcasted_iota(jnp.int32, (1, 128), 1)
    told = []
    for k in range(groups):
        mine = source // dp == (me ^ k)
        total = jnp.sum(jnp.where(mine, squares[...], 0), axis=0, keepdims=True)
        code = jnp.sum(jnp.where(source == (me ^ k) * dp, squares[...], 0), axis=0, keepdims=True)
        told.append(jnp.where(lane < rows, lax.rsqrt(total / width + EPS_OUT), code))
    told.append(jnp.zeros((128 - groups, 128), F32))
    scales[...] = jnp.concatenate(told, axis=0).T


def pack_kernel(*refs):
    *parts, out = refs
    rows = parts[0].shape[0] // 2
    for n, part in enumerate(parts):
        out[n * rows : (n + 1) * rows, :] = part[rows:, :]


def scaled(cap, size, k, rows, scales, gain):
    out = []
    for r in range(cap):
        inverse = scales[r * size : (r + 1) * size, k : k + 1]
        out.append((rows[r * size : (r + 1) * size, :].astype(F32) * inverse * gain).astype(BF16))
    return out


def moves(seq_len, cap, size, senders, scales):
    at = cap * size
    codes = [
        jnp.broadcast_to(scales[at + r : at + r + 1, k : k + 1], TILE)
        for k in senders
        for r in range(cap)
        for _ in range(size // 8)
    ]
    code = jnp.concatenate(codes, axis=0).T[0:1, :].astype(jnp.int32)
    position = lax.broadcasted_iota(jnp.int32, code.shape, 1) % size
    target = jnp.where(code > 0, (code - 1) * size + position, -1)
    return (lax.broadcasted_iota(jnp.int32, (seq_len, code.shape[1]), 0) == target).astype(F32)


def base_kernel(groups, dp, cap, size, width, squares, text_scale, gain, text, *rest):
    *even, out, scales, rows, done, sems = rest
    scale_kernel(groups, dp, cap * size, width, squares, scales)
    seq_len = text.shape[0]
    g = gain[...]
    order = moves(seq_len, cap, size, range(0, groups, 2), scales)
    covered = jnp.sum(order, axis=1, keepdims=True)
    for n, part in enumerate(even):
        for r, x in enumerate(scaled(cap, size, 2 * n, part, scales, g)):
            at = (n * cap + r) * size
            rows[at : at + size, :] = x
    moved = jnp.dot(order.astype(BF16), rows[...], preferred_element_type=F32)
    copies, stretch = [], seq_len // sems.shape[0]
    for c in range(seq_len // 16):
        inverse = jnp.concatenate([text_scale[:, 2 * c : 2 * c + 1], text_scale[:, 2 * c + 1 : 2 * c + 2]], axis=0)
        part = slice(c * 16, (c + 1) * 16)
        x = text[part, :].astype(F32) * inverse * g
        done[part, :] = jnp.where(covered[part] > 0, moved[part], x).astype(BF16)
        if (c + 1) * 16 % stretch == 0:
            there = slice((c + 1) * 16 - stretch, (c + 1) * 16)
            copies.append(pltpu.make_async_copy(done.at[there], out.at[there], sems.at[len(copies)]))
            copies[-1].start()
    for copy in copies:
        copy.wait()


def place_kernel(groups, cap, size, scales, gain, odd, base, out, done, sems):
    del base
    at = cap * size
    g = gain[...]
    places = [(n, k, r) for n, k in enumerate(range(1, groups, 2)) for r in range(cap)]
    starts = [jnp.sum(scales[at + r : at + r + 1, k : k + 1]).astype(jnp.int32) - 1 for _, k, r in places]

    def copy(m):
        there = pl.ds(pl.multiple_of(starts[m] * size, size), size)
        return pltpu.make_async_copy(done.at[m * size : (m + 1) * size], out.at[there], sems.at[m])

    for m, (n, k, r) in enumerate(places):
        if r == 0:
            rows = scaled(cap, size, k, odd[n * at : (n + 1) * at], scales, g)
        done[m * size : (m + 1) * size, :] = rows[r]

        @pl.when(starts[m] >= 0)
        def _():
            copy(m).start()

    for m in range(len(places)):

        @pl.when(starts[m] >= 0)
        def _():
            copy(m).wait()


def outer(x):
    return lax.ppermute(x, "dp", [(0, 1), (1, 0), (2, 3), (3, 2)])


def inner(x):
    return lax.ppermute(x, "dp", [(1, 2), (2, 1), (0, 0), (3, 3)])


def ends(x):
    return lax.ppermute(x, "dp", [(0, 3), (3, 0), (1, 1), (2, 2)])


def mirror(x):
    return lax.ppermute(x, "dp", [(0, 3), (1, 2), (2, 1), (3, 0)])


def second(x):
    return lax.ppermute(x, "dp", [(0, 2), (1, 3), (2, 0), (3, 1)])


def far(x):
    return lax.ppermute(x, "dp", [(0, 2), (1, 0), (2, 3), (3, 1)])


def across(x, k):
    return lax.ppermute(x, "grp", [(i, i ^ k) for i in range(lax.axis_size("grp"))])


def fast(vis, vis_gain, weight, bias, text, out_gain, counts, owners, offsets):
    groups, dp = lax.axis_size("grp"), lax.axis_size("dp")
    devices = groups * dp
    slots = owners.shape[0]
    size = vis.shape[0] // slots
    seq_len, columns = text.shape
    cap = seq_len // (groups * size)
    depth = vis.shape[1]
    small = pltpu.CompilerParams(vmem_limit_bytes=LIMIT)
    count = slots * size
    tile = jax.ShapeDtypeStruct(TILE, F32)
    bias = bias[None, :]

    x_inner, x_outer = inner(vis), outer(vis)
    info, own, held = pl.pallas_call(
        functools.partial(tables_kernel, slots, size),
        in_specs=[VMEM, VMEM, SMEM, SMEM, SMEM],
        out_specs=[VMEM] * 3,
        out_shape=[tile, jax.ShapeDtypeStruct(vis.shape, BF16), tile],
        compiler_params=small,
        name="tables",
    )(text, vis, owners, offsets, counts)
    x_ends = ends(vis)
    weight = pltpu.with_memory_space_constraint(weight, pltpu.VMEM)
    held = pl.pallas_call(
        hold_kernel,
        in_specs=[ANY, VMEM],
        out_specs=VMEM,
        out_shape=tile,
        compiler_params=small,
        cost_estimate=pl.CostEstimate(flops=0, bytes_accessed=2 * weight.size, transcendentals=0),
        name="hold",
    )(weight, held)
    x_inner, held = lax.optimization_barrier((x_inner, held))
    stretches = depth // 3 // 128 * 128
    stretches = (depth - stretches, stretches)
    stretch = depth // 4 // 128 * 128
    sent, later = pl.pallas_call(
        pass_kernel,
        in_specs=[VMEM] * 3,
        out_specs=[VMEM] * 2,
        out_shape=[jax.ShapeDtypeStruct((count, n), BF16) for n in (depth - stretch, stretch)],
        compiler_params=small,
        name="pass",
    )(own, x_inner, vis_gain)
    sent, later, x_outer = lax.optimization_barrier((sent, later, x_outer))
    last_a = far(sent)
    known = (second(info), mirror(info), outer(info), info)
    last_b = far(later)
    cost = pl.CostEstimate(
        flops=2 * 3 * count * depth * columns, bytes_accessed=2 * weight.size, transcendentals=0
    )
    early = pl.pallas_call(
        early_kernel,
        in_specs=[VMEM] * 7,
        out_specs=VMEM,
        out_shape=jax.ShapeDtypeStruct((3 * count, columns), BF16),
        scratch_shapes=[pltpu.VMEM((3 * count, depth), BF16)],
        compiler_params=small,
        cost_estimate=pl.CostEstimate(flops=0, bytes_accessed=0, transcendentals=0),
        name="early",
    )(own, x_outer, x_inner, x_ends, vis_gain, weight, bias)
    pairs = groups // 2
    total = pl.pallas_call(
        late_kernel,
        in_specs=[VMEM] * 3,
        out_specs=VMEM,
        out_shape=jax.ShapeDtypeStruct((count, columns), F32),
        compiler_params=small,
        cost_estimate=pl.CostEstimate(flops=0, bytes_accessed=0, transcendentals=0),
        name="late",
    )(last_a, weight, bias)
    *parts, squares, text_scale = pl.pallas_call(
        functools.partial(project_kernel, groups, cap, size, columns * dp),
        in_specs=[VMEM] * 9,
        out_specs=[VMEM] * (pairs + 2),
        out_shape=[jax.ShapeDtypeStruct((2 * cap * size, columns), BF16)] * pairs
        + [jax.ShapeDtypeStruct((devices, 128), F32), tile],
        scratch_shapes=[
            pltpu.VMEM((dp * count, columns), BF16),
            pltpu.VMEM((count, columns), BF16),
            pltpu.VMEM((dp * count, 128), F32),
        ],
        compiler_params=small,
        cost_estimate=cost,
        name="project",
    )(*known, last_b, weight, total, early, held)
    squares = lax.all_to_all(squares, ("grp", "dp"), 0, 0, tiled=True)
    even = [parts[0]] + [across(parts[j], 2 * j) for j in range(pairs - 1, 0, -1)][::-1]
    *even, squares = lax.optimization_barrier((*even, squares))
    arrived = jax.ShapeDtypeStruct((pairs * cap * size, columns), BF16)
    odd = pl.pallas_call(
        pack_kernel, in_specs=[VMEM] * pairs, out_specs=VMEM, out_shape=arrived, compiler_params=small, name="pack"
    )(*even)
    odd = across(odd, 1)
    gain = out_gain[None, :]
    base, scales = pl.pallas_call(
        functools.partial(base_kernel, groups, dp, cap, size, columns * dp),
        in_specs=[VMEM] * (4 + pairs),
        out_specs=[ANY, VMEM],
        out_shape=[jax.ShapeDtypeStruct(text.shape, BF16), jax.ShapeDtypeStruct((128, 128), F32)],
        scratch_shapes=[pltpu.VMEM(arrived.shape, BF16), pltpu.VMEM(text.shape, BF16), pltpu.SemaphoreType.DMA((4,))],
        compiler_params=small,
        cost_estimate=pl.CostEstimate(flops=0, bytes_accessed=2 * weight.size, transcendentals=0),
        name="base",
    )(squares, text_scale, gain, text, *even)
    return pl.pallas_call(
        functools.partial(place_kernel, groups, cap, size),
        in_specs=[VMEM] * 3 + [ANY],
        out_specs=ANY,
        out_shape=jax.ShapeDtypeStruct(text.shape, BF16),
        input_output_aliases={3: 0},
        scratch_shapes=[pltpu.VMEM(arrived.shape, BF16), pltpu.SemaphoreType.DMA((pairs * cap,))],
        compiler_params=small,
        name="place",
    )(scales, gain, odd, base)


def general(
    vis_features, vis_gain, proj_weight, proj_bias, text_embed, out_gain, image_counts, owner_block, offsets
):
    groups = lax.axis_size("grp")
    width = proj_weight.shape[1] * lax.axis_size("dp")
    slots_device = owner_block.shape[0]
    per_image = vis_features.shape[0] // slots_device
    columns = proj_weight.shape[1]
    seq_len = text_embed.shape[0]
    capacity = seq_len // (groups * per_image)
    features_f = vis_features.astype(jnp.float32)
    normed = (
        features_f
        * lax.rsqrt(jnp.mean(features_f * features_f, axis=-1, keepdims=True) + EPS_VIS)
        * vis_gain
    ).astype(jnp.bfloat16)
    slot_local = jnp.arange(slots_device, dtype=jnp.int32)
    live_offsets = jnp.where(slot_local < image_counts[0], offsets, -1)
    block_owner, block_offsets = (
        lax.all_gather(owner_block, "dp", axis=0, tiled=True),
        lax.all_gather(live_offsets, "dp", axis=0, tiled=True),
    )
    projected = (
        jnp.dot(
            lax.all_gather(normed, "dp", axis=0, tiled=True),
            proj_weight,
            preferred_element_type=jnp.float32,
        )
        + proj_bias
    ).astype(jnp.bfloat16)
    block_slots = block_owner.shape[0]
    earlier = jnp.arange(block_slots)[:, None] > jnp.arange(block_slots)[None, :]
    same_owner = block_owner[:, None] == block_owner[None, :]
    rank_in = jnp.sum(same_owner & earlier, axis=1)
    bucket = block_owner * capacity + rank_in
    selector = jnp.arange(groups * capacity, dtype=jnp.int32)[:, None] == bucket[None, :]
    flat_rows = projected.reshape(block_slots, per_image * columns)
    bucketed = jnp.dot(
        selector.astype(jnp.bfloat16), flat_rows, preferred_element_type=jnp.float32
    ).astype(jnp.bfloat16)
    bucketed = bucketed.reshape(groups, capacity * per_image * columns)
    bucket_offsets = jnp.max(jnp.where(selector, block_offsets[None, :], -1), axis=1).reshape(
        groups, capacity
    )
    arrived, arrived_offsets = (
        lax.all_to_all(bucketed, "grp", split_axis=0, concat_axis=0, tiled=True),
        lax.all_to_all(bucket_offsets, "grp", split_axis=0, concat_axis=0, tiled=True),
    )
    received = arrived.reshape(groups * capacity * per_image, columns)
    starts = arrived_offsets.reshape(groups * capacity)
    target = jnp.where(
        starts[:, None] >= 0,
        starts[:, None] + jnp.arange(per_image, dtype=jnp.int32)[None, :],
        seq_len,
    )
    target = target.reshape(-1).astype(jnp.int32)
    merged = text_embed.at[target].set(received, mode="drop")
    local_squares = jnp.sum(jnp.square(merged.astype(jnp.float32)), axis=1)
    row_total = lax.psum(local_squares, "dp")
    inverse_rms = lax.rsqrt(row_total / width + EPS_OUT)
    hidden = merged.astype(jnp.float32) * inverse_rms[:, None] * out_gain
    return hidden.astype(jnp.bfloat16)


def on_device(vis, vis_gain, weight, bias, text, out_gain, counts, owners, offsets):
    groups, dp = lax.axis_size("grp"), lax.axis_size("dp")
    per_image = vis.shape[0] // owners.shape[0]
    cap = text.shape[0] // (groups * per_image)
    full = dp * owners.shape[0] == groups * cap and groups * cap * per_image == text.shape[0]
    fits = dp == 4 and groups & (groups - 1) == 0 and per_image == 16 and cap == 2 and text.shape[0] <= 512 and 3 * owners.shape[0] <= TEXT
    fits = fits and owners.shape[0] % 4 == 0 and weight.shape[1] % 1024 == 0
    form = fast if full and fits else general
    return form(vis, vis_gain, weight, bias, text, out_gain, counts, owners, offsets)


def solution(mesh):
    return jax.shard_map(
        on_device,
        mesh=mesh,
        in_specs=(
            P(("grp", "dp"), None),
            P(),
            P(None, "dp"),
            P("dp"),
            P("grp", "dp"),
            P("dp"),
            P(("grp", "dp")),
            P(("grp", "dp")),
            P(("grp", "dp")),
        ),
        out_specs=P("grp", "dp"),
        check_vma=False,
    )
```
